512 devices in a mesh: section: 2 (over core), vocab: 64 (over z, x, y_lo), tok: 4 (over y_hi).
Axes of the slice: x: 4, y: 8 (y_hi: 4, y_lo: 2; y = y_hi * 2 + y_lo), z: 8, core: 2. Of those that a mesh axis runs over, the one named last changes fastest.
Arguments:
- rows: bfloat16 [2, 512, 3584], P('section', 'tok', 'vocab'), may hold values from -7 to 7
- targets: int32 [2, 512], P('section', 'tok'), may hold values from 0 to 65535
- proj_weight: bfloat16 [7168, 3584], P(None, 'vocab'), may hold values from -0.0625 to 0.0625
- head_weight: bfloat16 [3584, 65536], P(('section', 'tok'), 'vocab'), may hold values from -1 to 1
Outputs:
- head_grad: bfloat16 [3584, 65536], P(('section', 'tok'), 'vocab')
- hidden_grad: float32 [512, 3584], P('tok', 'vocab')
The draws below stay inside these ranges and needn't reach their ends.
All inputs are finite; a program needn't handle non-finite values.
Results may differ from the reference program's by a relative error of at most 0.0052.
Values may be sent and summed in bfloat16 or wider, within the bound.
A program may use at most 64 MiB of HBM per device.

```python
import math
import jax
import jax.numpy as jnp
from jax import lax

D = 3584
VOCAB = 65536
TOKENS = 512


def common_rows(key):
    normal_rows = jnp.clip(jax.random.normal(jax.random.fold_in(key, 101), (TOKENS, D), jnp.float32), -4.0, 4.0)
    return normal_rows


def draw_rows(key, part):
    normal_rows = common_rows(key)
    key = jax.random.fold_in(key, 1)
    hidden = normal_rows
    embed = jnp.clip(jax.random.normal(key, (TOKENS, D), jnp.float32), -4.0, 4.0)
    return jnp.stack([hidden, embed]).astype(jnp.bfloat16)


def draw_head_weight(key, part):
    key = jax.random.fold_in(key, 2)
    weights = jnp.clip(jax.random.normal(key, (D, VOCAB), jnp.float32), -6.0, 6.0) * (3.0 / math.sqrt(D))
    return weights.astype(jnp.bfloat16)


def set_ends(drawn, key, low, high):
    place = [jax.random.randint(jax.random.fold_in(key, axis), (), 0, length) for axis, length in enumerate(drawn.shape)]
    longest = drawn.shape.index(max(drawn.shape))
    beside = place[:longest] + [(place[longest] + 1) % drawn.shape[longest]] + place[longest + 1:]
    return drawn.at[tuple(place)].set(low).at[tuple(beside)].set(high)


def block_levels(stream_key, shape, cuts, smallest, high):
    loudness = 1.0
    for dim, blocks in cuts:
        steps = jax.random.uniform(jax.random.fold_in(jax.random.fold_in(stream_key, 6), dim), (blocks,), jnp.float32, smallest / len(cuts), high / len(cuts))
        loudness = loudness * jnp.repeat(jnp.exp(steps), shape[dim] // blocks).reshape((-1,) + (1,) * (len(shape) - 1 - dim))
    return loudness


def centred(stream_key, extent, spread, limit, cuts=(), kind=jnp.bfloat16):
    result = spread * jax.random.normal(stream_key, extent, jnp.float32)
    if cuts:
        result = result * block_levels(stream_key, extent, cuts, -0.22, 0.18)
    return jnp.clip(result, -limit, limit).astype(kind)


def setup_inputs(seed: int = 0) -> dict:
    splits = jax.random.split(jax.random.key(seed), 5)
    rows = draw_rows(jax.random.fold_in(splits[4], 71), 0)
    targets = set_ends(jax.random.randint(splits[1], (2, TOKENS), 0, VOCAB), jax.random.fold_in(splits[1], 1), 0, VOCAB - 1).astype(jnp.int32)
    proj_weight = centred(splits[2], (2 * D, D), (2 * D) ** -0.5, 0.0625, ((1, 64),))
    head_weight = draw_head_weight(jax.random.fold_in(splits[4], 71), 0)
    return {"rows": rows, "targets": targets, "proj_weight": proj_weight, "head_weight": head_weight}


EPS = 1e-06
MTP_WEIGHT = 0.3

def normalize(inputs):
    values = inputs.astype(jnp.float32)
    inverse = lax.rsqrt(lax.optimization_barrier(jnp.mean(values * values, axis=-1, keepdims=True)) + EPS)
    return (values * inverse, inverse)

def norm_backward(upstream, normed, rounded, inverse):
    row_dot = lax.optimization_barrier(jnp.mean(upstream * rounded.astype(jnp.float32), axis=-1, keepdims=True))
    return (upstream - normed * row_dot) * inverse

def head_pass(inputs, labels, weighting, head_weight):
    normed, inverse = normalize(inputs)
    rounded = normed.astype(jnp.bfloat16)
    logits = jnp.dot(rounded, head_weight, preferred_element_type=jnp.float32)
    probabilities = jax.nn.softmax(logits, axis=-1)
    columns = jnp.arange(logits.shape[1], dtype=jnp.int32)
    onehot = (columns[None, :] == labels[:, None]).astype(jnp.float32)
    logit_grad = (weighting * (probabilities - onehot)).astype(jnp.bfloat16)
    feature_grad = jnp.dot(logit_grad, head_weight.T, preferred_element_type=jnp.float32)
    return (rounded, logit_grad, norm_backward(feature_grad, normed, rounded, inverse))

def reference(rows, targets, proj_weight, head_weight):
    model_width = rows.shape[2]
    hidden_norm, hidden_inv = normalize(rows[0])
    embed_norm = normalize(rows[1])[0]
    joined = jnp.concatenate([hidden_norm, embed_norm], axis=1).astype(jnp.bfloat16)
    mixed_rows = jnp.dot(joined, proj_weight, preferred_element_type=jnp.float32).astype(jnp.bfloat16)
    main_rows, main_grad, main_back = head_pass(rows[0], targets[0], 1.0, head_weight)
    depth_rows, depth_grad, depth_back = head_pass(mixed_rows, targets[1], MTP_WEIGHT, head_weight)
    all_rows = jnp.concatenate([main_rows, depth_rows], axis=0)
    all_grads = jnp.concatenate([main_grad, depth_grad], axis=0)
    head_grad = lax.dot_general(all_rows, all_grads, (((0,), (0,)), ((), ())), preferred_element_type=jnp.float32).astype(jnp.bfloat16)
    mixed_grad = depth_back.astype(jnp.bfloat16)
    joined_grad = jnp.dot(mixed_grad, proj_weight[:model_width].T, preferred_element_type=jnp.float32)
    depth_hidden = norm_backward(joined_grad, hidden_norm, joined[:, :model_width], hidden_inv)
    return (head_grad, main_back + depth_hidden)
```

```python
import jax
import jax.numpy as jnp
from jax import lax
from jax.experimental import pallas as pl
from jax.experimental.pallas import tpu as pltpu
from jax.sharding import PartitionSpec as P

EPS = 1e-06
MTP_WEIGHT = 0.3
D = 3584
T = 128
C = 56
CP = 64
VS = 1024
KB = 448
MESH = pl.DeviceIdType.MESH
BF = jnp.bfloat16
F32 = jnp.float32


def rcopy(src, dst, ssem, rsem, dev):
    copy = pltpu.make_async_remote_copy(
        src_ref=src, dst_ref=dst, send_sem=ssem, recv_sem=rsem, device_id=dev, device_id_type=MESH
    )
    copy.start()


def await_bytes(ref, sem):
    pltpu.make_async_copy(ref, ref, sem).wait()


def kernel(
    rows_ref, lab_ref, proj_ref, w_ref, hg_ref, out_ref,
    wf, proj, ga, gb, normed, rt, rnd, logt, lg_all, r_all,
    p3, rx3, az3, af3, rz3, by3, ry3,
    p4, rx4, az4, af4, rz4, by4, ry4,
    sx, sz, sy, hx, hz, hy,
    xch, xin, bk, bkin,
    loc_sem, w_s, w_r, l_s, l_r, r_s, r_r,
    g1s, g1r, g2s, g2r, st_s, st_r, h_s, h_r, q3s, q3r, q4s, q4r, x_s, x_r,
):
    s = lax.axis_index("section")
    v = lax.axis_index("vocab")
    t = lax.axis_index("tok")
    z = lax.div(v, 8)
    x = lax.rem(lax.div(v, 2), 4)
    yl = lax.rem(v, 2)
    b = s * 4 + t
    sib = {"section": 1 - s}
    t_right = lax.rem(t + 1, 4)
    t_left = lax.rem(t + 3, 4)
    t_far = lax.rem(t + 2, 4)

    def at_z(d):
        return {"vocab": lax.rem(z + d, 8) * 8 + x * 2 + yl}

    def at_x(d):
        return {"vocab": z * 8 + lax.rem(x + d, 4) * 2 + yl}

    at_y = {"vocab": z * 8 + x * 2 + (1 - yl)}

    barrier = pltpu.get_barrier_semaphore()
    for d in range(1, 8):
        pl.semaphore_signal(barrier, inc=1, device_id=at_z(d), device_id_type=MESH)
    for d in range(1, 4):
        pl.semaphore_signal(barrier, inc=1, device_id=at_x(d), device_id_type=MESH)
    pl.semaphore_signal(barrier, inc=1, device_id=at_y, device_id_type=MESH)
    for d in range(1, 8):
        o = lax.rem(b + d, 8)
        pl.semaphore_signal(
            barrier, inc=1, device_id={"section": lax.div(o, 4), "tok": lax.rem(o, 4)}, device_id_type=MESH
        )
    ga[z, x, yl] = rows_ref[...]
    pl.semaphore_wait(barrier, 18)

    def gather(g, ss, rs):
        rcopy(g.at[z, x, yl], g.at[z, x, yl], ss.at[0], rs.at[0], at_y)
        await_bytes(g.at[z, x, 1 - yl], rs.at[0])
        for d in (4, 3, 5, 2, 6, 1, 7):
            rcopy(g.at[z, x], g.at[z, x], ss.at[1], rs.at[1], at_z(d))
        await_bytes(g.at[pl.ds(0, 7), x], rs.at[1])
        xl = lax.rem(x + 3, 4)
        xr = lax.rem(x + 1, 4)
        rcopy(g.at[:, x], g.at[:, x], ss.at[2], rs.at[2], at_x(1))
        rcopy(g.at[:, x], g.at[:, x], ss.at[2], rs.at[3], at_x(3))
        await_bytes(g.at[:, xl], rs.at[2])
        lo = pl.ds(0, 4)
        hi = pl.ds(4, 4)
        rcopy(g.at[lo, xl], g.at[lo, xl], ss.at[2], rs.at[4], at_x(1))
        await_bytes(g.at[:, xr], rs.at[3])
        rcopy(g.at[hi, xr], g.at[hi, xr], ss.at[2], rs.at[5], at_x(3))
        await_bytes(g.at[lo, x], rs.at[4])
        await_bytes(g.at[hi, x], rs.at[5])

    def gather_sent(g, ss):
        await_bytes(g.at[z, x, yl], ss.at[0])
        await_bytes(g.at[pl.ds(0, 7), x], ss.at[1])
        await_bytes(g.at[:, pl.ds(0, 3)], ss.at[2])

    def ring_start(own, piece, ss, rs):
        right = {"tok": t_right}
        left = {"tok": t_left}
        rcopy(own(0), piece(b, 0), ss, rs.at[0], right)
        rcopy(own(1), piece(b, 1), ss, rs.at[3], left)
        rcopy(own(0), piece(b, 0), ss, rs.at[6], sib)
        rcopy(own(1), piece(b, 1), ss, rs.at[6], sib)
        rcopy(own(1), piece(b, 1), ss, rs.at[1], right)
        rcopy(own(0), piece(b, 0), ss, rs.at[2], left)

    def hand(piece, blk, h, ss, rs):
        rcopy(piece(blk, h), piece(blk, h), ss, rs.at[6], sib)

    def ring_mid(piece, ss, rs):
        bl = s * 4 + t_left
        br = s * 4 + t_right
        await_bytes(piece(bl, 0), rs.at[0])
        rcopy(piece(bl, 0), piece(bl, 0), ss, rs.at[4], {"tok": t_right})
        await_bytes(piece(br, 1), rs.at[3])
        rcopy(piece(br, 1), piece(br, 1), ss, rs.at[5], {"tok": t_left})
        hand(piece, bl, 0, ss, rs)
        hand(piece, br, 1, ss, rs)

    def ring_late(piece, ss, rs):
        bl = s * 4 + t_left
        br = s * 4 + t_right
        bf = s * 4 + t_far
        await_bytes(piece(bl, 1), rs.at[1])
        hand(piece, bl, 1, ss, rs)
        await_bytes(piece(br, 0), rs.at[2])
        hand(piece, br, 0, ss, rs)
        await_bytes(piece(bf, 0), rs.at[4])
        hand(piece, bf, 0, ss, rs)
        await_bytes(piece(bf, 1), rs.at[5])
        hand(piece, bf, 1, ss, rs)

    def w_own(h):
        return w_ref.at[pl.ds(224 * h, 224), :]

    def w_piece(blk, h):
        return wf.at[pl.ds(pl.multiple_of(KB * blk + 224 * h, 32), 224), :]

    def l_piece(blk, h):
        return lg_all.at[pl.ds(512 * h, 512), pl.ds(pl.multiple_of(blk * T, T), T)]

    def l_own(h):
        return l_piece(b, h)

    pcopy = pltpu.make_async_copy(proj_ref, proj, loc_sem.at[0])
    pcopy.start()
    ring_start(w_own, w_piece, w_s, w_r)
    wcopy = pltpu.make_async_copy(w_ref, wf.at[pl.ds(pl.multiple_of(KB * b, 64), KB), :], loc_sem.at[1])
    wcopy.start()

    def normalize(g):
        def add(i, acc):
            for j in range(8):
                blk = g[i, j // 2, j % 2][:C, :].astype(F32)
                acc = acc + (blk * blk)
            return acc

        total = lax.fori_loop(0, 8, add, jnp.zeros((C, T), F32))
        inv = lax.rsqrt(jnp.sum(total, axis=0, keepdims=True) * (1.0 / D) + EPS)

        def scale(i, carry):
            parts = [g[i, j // 2, j % 2][:C, :].astype(F32) for j in range(8)]
            block = jnp.concatenate(parts, axis=0) * inv
            r = pl.multiple_of(i * KB, KB)
            normed[pl.ds(r, KB), :] = block
            rt[pl.ds(r, KB), :] = block.astype(BF)
            return carry

        lax.fori_loop(0, 8, scale, 0)
        return inv

    gather(ga, g1s, g1r)
    inv1 = normalize(ga)
    pcopy.wait()
    part = lax.dot_general(
        proj[pl.ds(pl.multiple_of(s * D, D), D), :], rt[...], (((0,), (0,)), ((), ())),
        preferred_element_type=F32,
    )
    own_rows = pl.ds(pl.multiple_of(v * C, 8), C)

    @pl.when(s == 0)
    def _():
        xch[pl.ds(0, C), :] = part
        xch[pl.ds(C, 8), :] = jnp.broadcast_to(inv1, (8, T))
        xch[pl.ds(CP, C), :] = normed[own_rows, :]
        xch[pl.ds(CP + C, 8), :] = jnp.zeros((8, T), F32)
        rcopy(xch, xin, x_s.at[0], x_r.at[0], sib)
        sy[2] = jnp.broadcast_to(inv1, (8, T))
        ring_mid(w_piece, w_s, w_r)

    @pl.when(s == 1)
    def _():
        await_bytes(xin, x_r.at[0])
        mixed = part + xin[pl.ds(0, C), :]
        gb[z, x, yl] = jnp.concatenate([mixed, jnp.zeros((CP - C, T), F32)], axis=0).astype(BF)
        gather(gb, g2s, g2r)
        sy[2] = jnp.broadcast_to(normalize(gb), (8, T))
        ring_mid(w_piece, w_s, w_r)

    def turn(i, carry):
        r = pl.multiple_of(i * T, T)
        rnd[:, pl.ds(r, T)] = normed[pl.ds(r, T), :].T.astype(BF)
        return carry

    lax.fori_loop(0, D // T, turn, 0)
    ring_late(w_piece, w_s, w_r)
    wcopy.wait()
    await_bytes(wf.at[pl.ds(0, 4 * KB), :], w_r.at[6])

    def to_owner(d, carry):
        o = lax.rem(b + d, 8)
        rcopy(
            rt.at[pl.ds(pl.multiple_of(o * KB, 64), KB), :],
            r_all.at[:, pl.ds(pl.multiple_of(b * T, T), T)],
            r_s, r_r, {"section": lax.div(o, 4), "tok": lax.rem(o, 4)},
        )
        return carry

    def logits_tile(i, carry):
        r = pl.multiple_of(i * 256, 256)
        tile = jnp.dot(rnd[...], wf[:, pl.ds(r, 256)], preferred_element_type=F32)
        logt[pl.ds(r, 256), :] = tile.T
        return carry

    lax.fori_loop(0, 4, logits_tile, 0)
    r_all[:, pl.ds(pl.multiple_of(b * T, T), T)] = rt[pl.ds(pl.multiple_of(b * KB, 64), KB), :]

    label = lab_ref[...]
    place = lax.broadcasted_iota(jnp.int32, (VS, T), 0)
    hit = place == label
    values = logt[...]
    top = jnp.max(values, axis=0, keepdims=True)
    expo = jnp.exp(values - top)
    den = jnp.sum(expo, axis=0, keepdims=True)
    sel = jnp.sum(expo * values, axis=0, keepdims=True)
    lab = jnp.sum(jnp.where(hit, values, 0.0), axis=0, keepdims=True)

    def combine(slots):
        m = slots[0][0:1]
        for q in slots[1:]:
            m = jnp.maximum(m, q[0:1])
        d_ = jnp.zeros((1, T), F32)
        e_ = jnp.zeros((1, T), F32)
        l_ = jnp.zeros((1, T), F32)
        for q in slots:
            f = jnp.exp(q[0:1] - m)
            d_ = d_ + q[1:2] * f
            e_ = e_ + q[2:3] * f
            l_ = l_ + q[3:4]
        return jnp.concatenate([m, d_, e_, l_, jnp.zeros((4, T), F32)], axis=0)

    sx[x] = jnp.concatenate([top, den, sel, lab, jnp.zeros((4, T), F32)], axis=0)
    for d in (2, 1, 3):
        rcopy(sx.at[x], sx.at[x], st_s.at[0], st_r.at[0], at_x(d))
    await_bytes(sx.at[pl.ds(0, 3)], st_r.at[0])
    sz[z] = combine([sx[i] for i in range(4)])
    for d in (4, 3, 5, 2, 6, 1, 7):
        rcopy(sz.at[z], sz.at[z], st_s.at[1], st_r.at[1], at_z(d))
    await_bytes(sz.at[pl.ds(0, 7)], st_r.at[1])
    sy[yl] = combine([sz[i] for i in range(8)])
    rcopy(sy.at[yl], sy.at[yl], st_s.at[2], st_r.at[2], at_y)
    await_bytes(sy.at[1 - yl], st_r.at[2])
    stats = combine([sy[0], sy[1]])
    weighting = jnp.where(s == 1, MTP_WEIGHT, 1.0).astype(F32)
    inv_den = 1.0 / stats[1:2]
    mean_dot = weighting * (stats[2:3] * inv_den - stats[3:4]) * (1.0 / D)
    prob = jnp.exp(logt[...] - stats[0:1]) * inv_den
    lgt = (weighting * (prob - hit.astype(F32))).astype(BF)
    lg_all[:, pl.ds(pl.multiple_of(b * T, T), T)] = lgt
    ring_start(l_own, l_piece, l_s, l_r)

    pad = jnp.zeros((CP - C, T), F32)

    def spread(block, p, i):
        for j in range(8):
            p[i, j // 2, j % 2] = jnp.concatenate([block[C * j:C * (j + 1), :], pad], axis=0).astype(BF)

    def feature(i, carry):
        r = pl.multiple_of(i * KB, KB)
        block = jnp.dot(wf[pl.ds(r, KB), :], lgt, preferred_element_type=F32)
        spread(block, p3, i)
        return carry

    lax.fori_loop(0, 8, feature, 0)

    def scatter(p, rx, az, af, rz, by, ry, ss, rs):
        for d in (2, 1, 3):
            xo = lax.rem(x + d, 4)
            rcopy(p.at[:, xo], rx.at[x], ss.at[0], rs.at[0], at_x(d))

        def rest():
            await_bytes(rx.at[pl.ds(0, 3)], rs.at[0])

            def add(i, carry):
                for j in range(2):
                    a = p[i, x, j].astype(F32)
                    for d in range(1, 4):
                        a = a + rx[lax.rem(x + d, 4), i, j].astype(F32)
                    af[i, j] = a
                    az[i, j] = a.astype(BF)
                return carry

            lax.fori_loop(0, 8, add, 0)
            for d in (4, 3, 5, 2, 6, 1, 7):
                zo = lax.rem(z + d, 8)
                rcopy(az.at[zo], rz.at[z], ss.at[1], rs.at[1], at_z(d))
            await_bytes(rz.at[pl.ds(0, 7)], rs.at[1])
            for j in range(2):
                a = af[z, j]
                for d in range(1, 8):
                    a = a + rz[lax.rem(z + d, 8), j].astype(F32)
                by[j] = a
            rcopy(by.at[1 - yl], ry, ss.at[2], rs.at[2], at_y)
            await_bytes(ry, rs.at[2])
            return (by[yl] + ry[...])[:C, :]

        return rest

    def scatter_sent(rx, rz, ry, ss):
        await_bytes(rx.at[pl.ds(0, 3)], ss.at[0])
        await_bytes(rz.at[pl.ds(0, 7)], ss.at[1])
        await_bytes(ry, ss.at[2])

    rest = scatter(p3, rx3, az3, af3, rz3, by3, ry3, q3s, q3r)
    lax.fori_loop(1, 8, to_owner, 0)
    fgrad = rest()
    back = (fgrad - normed[own_rows, :] * mean_dot) * sy[2][0:1]

    def head_grad():
        await_bytes(r_all.at[:, pl.ds(0, 7 * T)], r_r)
        ring_late(l_piece, l_s, l_r)
        await_bytes(lg_all.at[:, pl.ds(0, 4 * T)], l_r.at[6])

        def tile(i, carry):
            r = pl.multiple_of(i * 256, 256)
            g = lax.dot_general(
                r_all[...], lg_all[pl.ds(r, 256), :], (((1,), (1,)), ((), ())), preferred_element_type=F32
            )
            hg_ref[:, pl.ds(r, 256)] = g.astype(BF)
            return carry

        lax.fori_loop(0, 4, tile, 0)

    @pl.when(s == 0)
    def _():
        bk[...] = back
        rcopy(bk, bkin, x_s.at[1], x_r.at[1], sib)
        ring_mid(l_piece, l_s, l_r)
        head_grad()
        await_bytes(bkin, x_r.at[1])
        out_ref[...] = back + bkin[...]
        await_bytes(xch, x_s.at[0])

    @pl.when(s == 1)
    def _():
        mg = back.astype(BF)

        def joined(i, carry):
            r = pl.multiple_of(i * KB, KB)
            block = jnp.dot(proj[pl.ds(r, KB), :], mg, preferred_element_type=F32)
            spread(block, p4, i)
            return carry

        lax.fori_loop(0, 8, joined, 0)
        rest4 = scatter(p4, rx4, az4, af4, rz4, by4, ry4, q4s, q4r)
        hdot = jnp.sum(mg.astype(F32) * xin[pl.ds(0, C), :], axis=0, keepdims=True)
        hx[x] = jnp.broadcast_to(hdot, (8, T))
        for d in (2, 1, 3):
            rcopy(hx.at[x], hx.at[x], h_s.at[0], h_r.at[0], at_x(d))
        ring_mid(l_piece, l_s, l_r)
        await_bytes(hx.at[pl.ds(0, 3)], h_r.at[0])
        hz[z] = hx[0] + hx[1] + hx[2] + hx[3]
        for d in (4, 3, 5, 2, 6, 1, 7):
            rcopy(hz.at[z], hz.at[z], h_s.at[1], h_r.at[1], at_z(d))
        jgrad = rest4()
        await_bytes(hz.at[pl.ds(0, 7)], h_r.at[1])
        tot = hz[0]
        for i in range(1, 8):
            tot = tot + hz[i]
        hy[yl] = tot
        rcopy(hy.at[yl], hy.at[yl], h_s.at[2], h_r.at[2], at_y)
        await_bytes(hy.at[1 - yl], h_r.at[2])
        hmean = (hy[0] + hy[1])[0:1] * (1.0 / D)
        depth = (jgrad - xin[pl.ds(CP, C), :] * hmean) * xin[pl.ds(C, 1), :]
        bk[...] = depth
        rcopy(bk, bkin, x_s.at[1], x_r.at[1], sib)
        await_bytes(bkin, x_r.at[1])
        out_ref[...] = bkin[...] + depth
        head_grad()
        gather_sent(gb, g2s)
        scatter_sent(rx4, rz4, ry4, q4s)
        await_bytes(hx.at[pl.ds(0, 3)], h_s.at[0])
        await_bytes(hz.at[pl.ds(0, 7)], h_s.at[1])
        await_bytes(hy.at[0], h_s.at[2])

    await_bytes(bk, x_s.at[1])
    gather_sent(ga, g1s)
    scatter_sent(rx3, rz3, ry3, q3s)
    await_bytes(sx.at[pl.ds(0, 3)], st_s.at[0])
    await_bytes(sz.at[pl.ds(0, 7)], st_s.at[1])
    await_bytes(sy.at[0], st_s.at[2])
    await_bytes(r_all.at[:, pl.ds(0, 7 * T)], r_s)
    await_bytes(wf.at[pl.ds(0, 7 * KB), :], w_s)
    await_bytes(lg_all.at[:, pl.ds(0, 7 * T)], l_s)


def local(rows, targets, proj_weight, head_weight):
    rows_t = jnp.pad(rows[0].T, ((0, CP - C), (0, 0)))
    labels = targets - lax.axis_index("vocab") * VS
    vm = pl.BlockSpec(memory_space=pltpu.VMEM)
    anyspace = pl.BlockSpec(memory_space=pl.ANY)
    dma = pltpu.SemaphoreType.DMA

    def rs_bufs():
        return [
            pltpu.VMEM((8, 4, 2, CP, T), BF),
            pltpu.VMEM((4, 8, 2, CP, T), BF),
            pltpu.VMEM((8, 2, CP, T), BF),
            pltpu.VMEM((8, 2, CP, T), F32),
            pltpu.VMEM((8, 2, CP, T), BF),
            pltpu.VMEM((2, CP, T), F32),
            pltpu.VMEM((CP, T), F32),
        ]

    head_grad, grad_t = pl.pallas_call(
        kernel,
        out_shape=(
            jax.ShapeDtypeStruct((KB, VS), BF),
            jax.ShapeDtypeStruct((C, T), F32),
        ),
        in_specs=[vm, vm, anyspace, anyspace],
        out_specs=(vm, vm),
        scratch_shapes=[
            pltpu.VMEM((D, VS), BF),
            pltpu.VMEM((2 * D, C), BF),
            pltpu.VMEM((8, 4, 2, CP, T), BF),
            pltpu.VMEM((8, 4, 2, CP, T), BF),
            pltpu.VMEM((D, T), F32),
            pltpu.VMEM((D, T), BF),
            pltpu.VMEM((T, D), BF),
            pltpu.VMEM((VS, T), F32),
            pltpu.VMEM((VS, 8 * T), BF),
            pltpu.VMEM((KB, 8 * T), BF),
            *rs_bufs(),
            *rs_bufs(),
            pltpu.VMEM((4, 8, T), F32),
            pltpu.VMEM((8, 8, T), F32),
            pltpu.VMEM((3, 8, T), F32),
            pltpu.VMEM((4, 8, T), F32),
            pltpu.VMEM((8, 8, T), F32),
            pltpu.VMEM((2, 8, T), F32),
            pltpu.VMEM((2 * CP, T), F32),
            pltpu.VMEM((2 * CP, T), F32),
            pltpu.VMEM((C, T), F32),
            pltpu.VMEM((C, T), F32),
            dma((2,)), dma, dma((7,)), dma, dma((7,)), dma, dma,
            dma((3,)), dma((6,)), dma((3,)), dma((6,)),
            dma((3,)), dma((3,)), dma((3,)), dma((3,)),
            dma((3,)), dma((3,)), dma((3,)), dma((3,)),
            dma((2,)), dma((2,)),
        ],
        compiler_params=pltpu.CompilerParams(
            collective_id=0, has_side_effects=True, vmem_limit_bytes=56 * 1024 * 1024
        ),
        cost_estimate=pl.CostEstimate(flops=3 * 10**9, bytes_accessed=2 * 10**7, transcendentals=3 * 10**5),
        name="head",
    )(rows_t, labels, proj_weight, head_weight)
    return head_grad, grad_t.T


def solution(mesh):
    placed = (
        P("section", "tok", "vocab"),
        P("section", "tok"),
        P(None, "vocab"),
        P(("section", "tok"), "vocab"),
    )
    return jax.shard_map(
        local,
        mesh=mesh,
        in_specs=placed,
        out_specs=(P(("section", "tok"), "vocab"), P("tok", "vocab")),
        check_vma=False,
    )
```

```python
import jax
import jax.numpy as jnp
from jax import lax
from jax.experimental import pallas as pl
from jax.experimental.pallas import tpu as pltpu
from jax.sharding import PartitionSpec as P

EPS = 1e-06
MTP_WEIGHT = 0.3
D = 3584
T = 128
C = 56
CP = 64
VS = 1024
KB = 448
MESH = pl.DeviceIdType.MESH
ORDER = (8, 7, 9, 6, 10, 5, 11, 4, 12, 3, 13, 2, 14, 1, 15)
GROUP = 2
GROUPS = 8 // GROUP
BF = jnp.bfloat16
F32 = jnp.float32


def rcopy(src, dst, ssem, rsem, dev):
    copy = pltpu.make_async_remote_copy(
        src_ref=src, dst_ref=dst, send_sem=ssem, recv_sem=rsem, device_id=dev, device_id_type=MESH
    )
    copy.start()


def await_bytes(ref, sem):
    pltpu.make_async_copy(ref, ref, sem).wait()


def kernel(
    rows_ref, lab_ref, proj_ref, w_ref, hg_ref, out_ref,
    wf, proj, ph, ga, gb, normed, rt, rnd, logt, lg_all, r_all,
    p3, rx3, az3, af3, rz3,
    p4, rx4, az4, af4, rz4,
    sx, sz, inv_keep, hx, hz,
    xch, xin, bk, bkin,
    loc_sem, w_s, w_r, l_s, l_r, r_s, r_r,
    g1s, g1r, g2s, g2r, st_s, st_r, h_s, h_r, q3s, q3r, q4s, q4r, x_s, x_r,
):
    s = lax.axis_index("section")
    v = lax.axis_index("vocab")
    t = lax.axis_index("tok")
    z = lax.div(v, 8)
    x = lax.rem(lax.div(v, 2), 4)
    yl = lax.rem(v, 2)
    b = s * 4 + t
    sib = {"section": 1 - s}
    t_right = lax.rem(t + 1, 4)
    t_left = lax.rem(t + 3, 4)
    t_far = lax.rem(t + 2, 4)

    def at_z(d):
        return {"vocab": lax.rem(z + d, 8) * 8 + x * 2 + yl}

    def at_x(d):
        return {"vocab": z * 8 + lax.rem(x + d, 4) * 2 + yl}

    zy = z * 2 + yl

    def vocab_of(e):
        return {"vocab": lax.div(e, 2) * 8 + x * 2 + lax.rem(e, 2)}

    def at_zy(d):
        return vocab_of(lax.rem(zy + d, 16))

    at_y = {"vocab": z * 8 + x * 2 + (1 - yl)}

    barrier = pltpu.get_barrier_semaphore()
    for d in range(1, 16):
        pl.semaphore_signal(barrier, inc=1, device_id=at_zy(d), device_id_type=MESH)
    for d in range(1, 4):
        pl.semaphore_signal(barrier, inc=1, device_id=at_x(d), device_id_type=MESH)
    for d in range(1, 8):
        o = lax.rem(b + d, 8)
        pl.semaphore_signal(
            barrier, inc=1, device_id={"section": lax.div(o, 4), "tok": lax.rem(o, 4)}, device_id_type=MESH
        )
    own_t = rows_ref[0].astype(F32)
    ga[z, x, yl] = jnp.concatenate([own_t, jnp.zeros((CP - C, T), F32)], axis=0).astype(BF)
    pl.semaphore_wait(barrier, 25)

    def gather_y(g, ss, rs):
        rcopy(g.at[z, x, yl], g.at[z, x, yl], ss.at[0], rs.at[0], at_y)
        await_bytes(g.at[z, x, 1 - yl], rs.at[0])

    def gather(g, ss, rs):
        for d in (4, 3, 5, 2, 6, 1, 7):
            rcopy(g.at[z, x], g.at[z, x], ss.at[1], rs.at[1], at_z(d))
        await_bytes(g.at[pl.ds(0, 7), x], rs.at[1])
        xl = lax.rem(x + 3, 4)
        xr = lax.rem(x + 1, 4)
        rcopy(g.at[:, x], g.at[:, x], ss.at[2], rs.at[2], at_x(1))
        rcopy(g.at[:, x], g.at[:, x], ss.at[2], rs.at[3], at_x(3))
        await_bytes(g.at[:, xl], rs.at[2])
        lo = pl.ds(0, 4)
        hi = pl.ds(4, 4)
        rcopy(g.at[lo, xl], g.at[lo, xl], ss.at[2], rs.at[4], at_x(1))
        await_bytes(g.at[:, xr], rs.at[3])
        rcopy(g.at[hi, xr], g.at[hi, xr], ss.at[2], rs.at[5], at_x(3))
        await_bytes(g.at[lo, x], rs.at[4])
        await_bytes(g.at[hi, x], rs.at[5])

    def gather_sent(g, ss):
        await_bytes(g.at[z, x, yl], ss.at[0])
        await_bytes(g.at[pl.ds(0, 7), x], ss.at[1])
        await_bytes(g.at[:, pl.ds(0, 3)], ss.at[2])

    def ring_start(own, piece, ss, rs):
        right = {"tok": t_right}
        left = {"tok": t_left}
        rcopy(own(0), piece(b, 0), ss, rs.at[0], right)
        rcopy(own(1), piece(b, 1), ss, rs.at[3], left)
        rcopy(own(0), piece(b, 0), ss, rs.at[6], sib)
        rcopy(own(1), piece(b, 1), ss, rs.at[6], sib)
        rcopy(own(1), piece(b, 1), ss, rs.at[1], right)
        rcopy(own(0), piece(b, 0), ss, rs.at[2], left)

    def hand(piece, blk, h, ss, rs):
        rcopy(piece(blk, h), piece(blk, h), ss, rs.at[6], sib)

    def ring_mid(piece, ss, rs):
        bl = s * 4 + t_left
        br = s * 4 + t_right
        await_bytes(piece(bl, 0), rs.at[0])
        rcopy(piece(bl, 0), piece(bl, 0), ss, rs.at[4], {"tok": t_right})
        await_bytes(piece(br, 1), rs.at[3])
        rcopy(piece(br, 1), piece(br, 1), ss, rs.at[5], {"tok": t_left})
        hand(piece, bl, 0, ss, rs)
        hand(piece, br, 1, ss, rs)

    def ring_late(piece, ss, rs):
        bl = s * 4 + t_left
        br = s * 4 + t_right
        bf = s * 4 + t_far
        await_bytes(piece(bl, 1), rs.at[1])
        hand(piece, bl, 1, ss, rs)
        await_bytes(piece(br, 0), rs.at[2])
        hand(piece, br, 0, ss, rs)
        await_bytes(piece(bf, 0), rs.at[4])
        hand(piece, bf, 0, ss, rs)
        await_bytes(piece(bf, 1), rs.at[5])
        hand(piece, bf, 1, ss, rs)

    def w_own(h):
        return w_ref.at[pl.ds(224 * h, 224), :]

    def w_piece(blk, h):
        return wf.at[pl.ds(pl.multiple_of(KB * blk + 224 * h, 32), 224), :]

    def l_piece(blk, h):
        return lg_all.at[pl.ds(512 * h, 512), pl.ds(pl.multiple_of(blk * T, T), T)]

    def l_own(h):
        return l_piece(b, h)

    pcopy = pltpu.make_async_copy(proj_ref, proj, loc_sem.at[0])
    pcopy.start()
    gather_y(ga, g1s, g1r)
    ring_start(w_own, w_piece, w_s, w_r)
    wcopy = pltpu.make_async_copy(w_ref, wf.at[pl.ds(pl.multiple_of(KB * b, 64), KB), :], loc_sem.at[1])
    wcopy.start()

    def normalize(g):
        def add(i, acc):
            for j in range(8):
                blk = g[i, j // 2, j % 2][:C, :].astype(F32)
                acc = acc + (blk * blk)
            return acc

        total = lax.fori_loop(0, 8, add, jnp.zeros((C, T), F32))
        inv = lax.rsqrt(jnp.sum(total, axis=0, keepdims=True) * (1.0 / D) + EPS)

        def scale(i, carry):
            parts = [g[i, j // 2, j % 2][:C, :].astype(F32) for j in range(8)]
            block = jnp.concatenate(parts, axis=0) * inv
            r = pl.multiple_of(i * KB, KB)
            normed[pl.ds(r, KB), :] = block
            rt[pl.ds(r, KB), :] = block.astype(BF)
            return carry

        lax.fori_loop(0, 8, scale, 0)
        return inv

    gather(ga, g1s, g1r)
    inv1 = normalize(ga)
    pcopy.wait()
    part = jnp.dot(proj[:, pl.ds(pl.multiple_of(s * D, D), D)], rt[...], preferred_element_type=F32)
    own_rows = pl.ds(pl.multiple_of(v * C, 8), C)

    @pl.when(s == 0)
    def _():
        xch[pl.ds(0, C), :] = part
        xch[pl.ds(C, 8), :] = jnp.broadcast_to(inv1, (8, T))
        xch[pl.ds(CP, C), :] = normed[own_rows, :]
        xch[pl.ds(CP + C, 8), :] = jnp.zeros((8, T), F32)
        rcopy(xch, xin, x_s.at[0], x_r.at[0], sib)
        inv_keep[...] = jnp.broadcast_to(inv1, (8, T))
        ring_mid(w_piece, w_s, w_r)

    @pl.when(s == 1)
    def _():
        await_bytes(xin, x_r.at[0])
        mixed = part + xin[pl.ds(0, C), :]
        gb[z, x, yl] = jnp.concatenate([mixed, jnp.zeros((CP - C, T), F32)], axis=0).astype(BF)
        gather_y(gb, g2s, g2r)
        gather(gb, g2s, g2r)
        inv_keep[...] = jnp.broadcast_to(normalize(gb), (8, T))
        ring_mid(w_piece, w_s, w_r)

    @pl.when(s == 1)
    def _():
        def turn_proj(i, carry):
            r = pl.multiple_of(i * T, T)
            ph[pl.ds(r, T), :] = proj[:, pl.ds(r, T)].astype(F32).T.astype(BF)
            return carry

        lax.fori_loop(0, D // T, turn_proj, 0)

    def turn(i, carry):
        r = pl.multiple_of(i * T, T)
        rnd[:, pl.ds(r, T)] = normed[pl.ds(r, T), :].T.astype(BF)
        return carry

    lax.fori_loop(0, D // T, turn, 0)
    ring_late(w_piece, w_s, w_r)
    wcopy.wait()
    await_bytes(wf.at[pl.ds(0, 4 * KB), :], w_r.at[6])

    def to_owner(d, carry):
        o = lax.rem(b + d, 8)
        rcopy(
            rt.at[pl.ds(pl.multiple_of(o * KB, 64), KB), :],
            r_all.at[:, pl.ds(pl.multiple_of(b * T, T), T)],
            r_s, r_r, {"section": lax.div(o, 4), "tok": lax.rem(o, 4)},
        )
        return carry

    def logits_tile(i, carry):
        r = pl.multiple_of(i * 256, 256)
        tile = jnp.dot(rnd[...], wf[:, pl.ds(r, 256)], preferred_element_type=F32)
        logt[pl.ds(r, 256), :] = tile.T
        return carry

    lax.fori_loop(0, 4, logits_tile, 0)
    r_all[:, pl.ds(pl.multiple_of(b * T, T), T)] = rt[pl.ds(pl.multiple_of(b * KB, 64), KB), :]

    label = lab_ref[...] - v * VS
    place = lax.broadcasted_iota(jnp.int32, (VS, T), 0)
    hit = place == label
    values = logt[...]
    top = jnp.max(values, axis=0, keepdims=True)
    expo = jnp.exp(values - top)
    den = jnp.sum(expo, axis=0, keepdims=True)
    sel = jnp.sum(expo * values, axis=0, keepdims=True)
    lab = jnp.sum(jnp.where(hit, values, 0.0), axis=0, keepdims=True)

    def combine(slots):
        m = slots[0][0:1]
        for q in slots[1:]:
            m = jnp.maximum(m, q[0:1])
        d_ = jnp.zeros((1, T), F32)
        e_ = jnp.zeros((1, T), F32)
        l_ = jnp.zeros((1, T), F32)
        for q in slots:
            f = jnp.exp(q[0:1] - m)
            d_ = d_ + q[1:2] * f
            e_ = e_ + q[2:3] * f
            l_ = l_ + q[3:4]
        return jnp.concatenate([m, d_, e_, l_, jnp.zeros((4, T), F32)], axis=0)

    sx[x] = jnp.concatenate([top, den, sel, lab, jnp.zeros((4, T), F32)], axis=0)
    for d in (2, 1, 3):
        rcopy(sx.at[x], sx.at[x], st_s.at[0], st_r.at[0], at_x(d))
    await_bytes(sx.at[pl.ds(0, 3)], st_r.at[0])
    sz[zy] = combine([sx[i] for i in range(4)])
    for d in ORDER:
        rcopy(sz.at[zy], sz.at[zy], st_s.at[1], st_r.at[1], at_zy(d))
    await_bytes(sz.at[pl.ds(0, 15)], st_r.at[1])
    stats = combine([sz[i] for i in range(16)])
    weighting = jnp.where(s == 1, MTP_WEIGHT, 1.0).astype(F32)
    inv_den = 1.0 / stats[1:2]
    mean_dot = weighting * (stats[2:3] * inv_den - stats[3:4]) * (1.0 / D)
    prob = jnp.exp(logt[...] - stats[0:1]) * inv_den
    lgt = (weighting * (prob - hit.astype(F32))).astype(BF)
    lg_all[:, pl.ds(pl.multiple_of(b * T, T), T)] = lgt
    ring_start(l_own, l_piece, l_s, l_r)

    pad = jnp.zeros((CP - C, T), F32)

    def spread(block, p, i):
        for j in range(8):
            p[i, j // 2, j % 2] = jnp.concatenate([block[C * j:C * (j + 1), :], pad], axis=0).astype(BF)

    def group(d):
        return lax.rem(lax.div(z, GROUP) + d, GROUPS)

    def blocks(d):
        return pl.ds(pl.multiple_of(group(d) * GROUP, GROUP), GROUP)

    def scatter_x(make, p, rx, ss, rs):
        for n in range(GROUPS):
            d = GROUPS - 1 - n
            for k in range(GROUP):
                make(group(d) * GROUP + k)
            for dx in (2, 1, 3):
                xo = lax.rem(x + dx, 4)
                rcopy(p.at[blocks(d), xo], rx.at[x, blocks(d)], ss, rs.at[d], at_x(dx))

    def scatter_zy(p, rx, az, af, rz, ss, rs, ss2, rs2):
        for n in range(GROUPS):
            d = GROUPS - 1 - n
            await_bytes(rx.at[pl.ds(0, 3), blocks(d)], rs.at[d])
            for k in range(GROUP):
                i = group(d) * GROUP + k
                for j in range(2):
                    a = p[i, x, j].astype(F32)
                    for dx in range(1, 4):
                        a = a + rx[lax.rem(x + dx, 4), i, j].astype(F32)
                    e = i * 2 + j
                    af[e] = a
                    az[e] = a.astype(BF)

                    @pl.when(e != zy)
                    def _():
                        rcopy(az.at[e], rz.at[zy], ss2, rs2, vocab_of(e))
        await_bytes(rz.at[pl.ds(0, 15)], rs2)
        a = af[zy]
        for d in range(1, 16):
            a = a + rz[lax.rem(zy + d, 16)].astype(F32)
        return a[:C, :]

    def scatter_sent(rx, rz, ss, ss2):
        await_bytes(rx.at[pl.ds(0, 3)], ss)
        await_bytes(rz.at[pl.ds(0, 15)], ss2)

    def feature(i):
        block = jnp.dot(wf[pl.ds(pl.multiple_of(i * KB, KB), KB), :], lgt, preferred_element_type=F32)
        spread(block, p3, i)

    scatter_x(feature, p3, rx3, q3s.at[0], q3r)
    lax.fori_loop(1, 8, to_owner, 0)
    fgrad = scatter_zy(p3, rx3, az3, af3, rz3, q3s.at[0], q3r, q3s.at[1], q3r.at[8])
    back = (fgrad - normed[own_rows, :] * mean_dot) * inv_keep[0:1]

    def head_grad():
        await_bytes(r_all.at[:, pl.ds(0, 7 * T)], r_r)
        ring_late(l_piece, l_s, l_r)
        await_bytes(lg_all.at[:, pl.ds(0, 4 * T)], l_r.at[6])

        def tile(i, carry):
            r = pl.multiple_of(i * 256, 256)
            g = lax.dot_general(
                r_all[...], lg_all[pl.ds(r, 256), :], (((1,), (1,)), ((), ())), preferred_element_type=F32
            )
            hg_ref[:, pl.ds(r, 256)] = g.astype(BF)
            return carry

        lax.fori_loop(0, 4, tile, 0)

    @pl.when(s == 0)
    def _():
        bk[...] = back
        rcopy(bk, bkin, x_s.at[1], x_r.at[1], sib)
        ring_mid(l_piece, l_s, l_r)
        head_grad()
        await_bytes(bkin, x_r.at[1])
        out_ref[...] = back + bkin[...]
        await_bytes(xch, x_s.at[0])

    @pl.when(s == 1)
    def _():
        mg = back.astype(BF)

        def joined(i):
            block = jnp.dot(ph[pl.ds(pl.multiple_of(i * KB, KB), KB), :], mg, preferred_element_type=F32)
            spread(block, p4, i)

        scatter_x(joined, p4, rx4, q4s.at[0], q4r)
        hdot = jnp.sum(mg.astype(F32) * xin[pl.ds(0, C), :], axis=0, keepdims=True)
        hx[x] = jnp.broadcast_to(hdot, (8, T))
        for d in (2, 1, 3):
            rcopy(hx.at[x], hx.at[x], h_s.at[0], h_r.at[0], at_x(d))
        ring_mid(l_piece, l_s, l_r)
        await_bytes(hx.at[pl.ds(0, 3)], h_r.at[0])
        hz[zy] = hx[0] + hx[1] + hx[2] + hx[3]
        for d in ORDER:
            rcopy(hz.at[zy], hz.at[zy], h_s.at[1], h_r.at[1], at_zy(d))
        jgrad = scatter_zy(p4, rx4, az4, af4, rz4, q4s.at[0], q4r, q4s.at[1], q4r.at[8])
        await_bytes(hz.at[pl.ds(0, 15)], h_r.at[1])
        tot = hz[0]
        for i in range(1, 16):
            tot = tot + hz[i]
        hmean = tot[0:1] * (1.0 / D)
        depth = (jgrad - xin[pl.ds(CP, C), :] * hmean) * xin[pl.ds(C, 1), :]
        bk[...] = depth
        rcopy(bk, bkin, x_s.at[1], x_r.at[1], sib)
        await_bytes(bkin, x_r.at[1])
        out_ref[...] = bkin[...] + depth
        head_grad()
        gather_sent(gb, g2s)
        scatter_sent(rx4, rz4, q4s.at[0], q4s.at[1])
        await_bytes(hx.at[pl.ds(0, 3)], h_s.at[0])
        await_bytes(hz.at[pl.ds(0, 15)], h_s.at[1])

    await_bytes(bk, x_s.at[1])
    gather_sent(ga, g1s)
    scatter_sent(rx3, rz3, q3s.at[0], q3s.at[1])
    await_bytes(sx.at[pl.ds(0, 3)], st_s.at[0])
    await_bytes(sz.at[pl.ds(0, 15)], st_s.at[1])
    await_bytes(r_all.at[:, pl.ds(0, 7 * T)], r_s)
    await_bytes(wf.at[pl.ds(0, 7 * KB), :], w_s)
    await_bytes(lg_all.at[:, pl.ds(0, 7 * T)], l_s)


def local(rows, targets, proj_weight, head_weight):
    vm = pl.BlockSpec(memory_space=pltpu.VMEM)
    anyspace = pl.BlockSpec(memory_space=pl.ANY)
    dma = pltpu.SemaphoreType.DMA

    def rs_bufs():
        return [
            pltpu.VMEM((8, 4, 2, CP, T), BF),
            pltpu.VMEM((4, 8, 2, CP, T), BF),
            pltpu.VMEM((16, CP, T), BF),
            pltpu.VMEM((16, CP, T), F32),
            pltpu.VMEM((16, CP, T), BF),
        ]

    head_grad, grad_t = pl.pallas_call(
        kernel,
        out_shape=(
            jax.ShapeDtypeStruct((KB, VS), BF),
            jax.ShapeDtypeStruct((C, T), F32),
        ),
        in_specs=[vm, vm, anyspace, anyspace],
        out_specs=(vm, vm),
        scratch_shapes=[
            pltpu.VMEM((D, VS), BF),
            pltpu.VMEM((C, 2 * D), BF),
            pltpu.VMEM((D, C), BF),
            pltpu.VMEM((8, 4, 2, CP, T), BF),
            pltpu.VMEM((8, 4, 2, CP, T), BF),
            pltpu.VMEM((D, T), F32),
            pltpu.VMEM((D, T), BF),
            pltpu.VMEM((T, D), BF),
            pltpu.VMEM((VS, T), F32),
            pltpu.VMEM((VS, 8 * T), BF),
            pltpu.VMEM((KB, 8 * T), BF),
            *rs_bufs(),
            *rs_bufs(),
            pltpu.VMEM((4, 8, T), F32),
            pltpu.VMEM((16, 8, T), F32),
            pltpu.VMEM((8, T), F32),
            pltpu.VMEM((4, 8, T), F32),
            pltpu.VMEM((16, 8, T), F32),
            pltpu.VMEM((2 * CP, T), F32),
            pltpu.VMEM((2 * CP, T), F32),
            pltpu.VMEM((C, T), F32),
            pltpu.VMEM((C, T), F32),
            dma((2,)), dma, dma((7,)), dma, dma((7,)), dma, dma,
            dma((3,)), dma((6,)), dma((3,)), dma((6,)),
            dma((2,)), dma((2,)), dma((2,)), dma((2,)),
            dma((2,)), dma((9,)), dma((2,)), dma((9,)),
            dma((2,)), dma((2,)),
        ],
        compiler_params=pltpu.CompilerParams(
            collective_id=0, has_side_effects=True, vmem_limit_bytes=56 * 1024 * 1024
        ),
        cost_estimate=pl.CostEstimate(flops=3 * 10**9, bytes_accessed=2 * 10**7, transcendentals=3 * 10**5),
        name="head",
    )(jnp.swapaxes(rows, 1, 2), targets, proj_weight.T, head_weight)
    return head_grad, grad_t.T


def solution(mesh):
    placed = (
        P("section", "tok", "vocab"),
        P("section", "tok"),
        P(None, "vocab"),
        P(("section", "tok"), "vocab"),
    )
    return jax.shard_map(
        local,
        mesh=mesh,
        in_specs=placed,
        out_specs=(P(("section", "tok"), "vocab"), P("tok", "vocab")),
        check_vma=False,
    )
```

```python
import jax
import jax.numpy as jnp
from jax import lax
from jax.experimental import pallas as pl
from jax.experimental.pallas import tpu as pltpu
from jax.sharding import PartitionSpec as P

EPS = 1e-06
MTP_WEIGHT = 0.3
D = 3584
T = 128
C = 56
CP = 64
VS = 1024
KB = 448
MESH = pl.DeviceIdType.MESH
ORDER = (8, 7, 9, 6, 10, 5, 11, 4, 12, 3, 13, 2, 14, 1, 15)
GROUP = 2
GROUPS = 8 // GROUP
BF = jnp.bfloat16
F32 = jnp.float32


def rcopy(src, dst, ssem, rsem, dev):
    copy = pltpu.make_async_remote_copy(
        src_ref=src, dst_ref=dst, send_sem=ssem, recv_sem=rsem, device_id=dev, device_id_type=MESH
    )
    copy.start()


def await_bytes(ref, sem):
    pltpu.make_async_copy(ref, ref, sem).wait()


def kernel(
    rows_ref, lab_ref, proj_ref, w_ref, hg_ref, out_ref,
    wf, proj, ph, ga, gb, normed, rt, rnd, logt, lg_all, r_all,
    p3, rx3, az3, af3, rz3,
    phr, pb, mgb, jb, jx, sx, sz, inv_keep,
    xch, xin, bk, bkin,
    loc_sem, w_s, w_r, l_s, l_r, r_s, r_r,
    g1s, g1r, g2s, g2r, st_s, st_r, q3s, q3r, p_s, p_r, m_s, m_r, j_s, j_r, x_s, x_r,
):
    s = lax.axis_index("section")
    v = lax.axis_index("vocab")
    t = lax.axis_index("tok")
    z = lax.div(v, 8)
    x = lax.rem(lax.div(v, 2), 4)
    yl = lax.rem(v, 2)
    b = s * 4 + t
    sib = {"section": 1 - s}
    t_right = lax.rem(t + 1, 4)
    t_left = lax.rem(t + 3, 4)
    t_far = lax.rem(t + 2, 4)

    def at_z(d):
        return {"vocab": lax.rem(z + d, 8) * 8 + x * 2 + yl}

    def at_x(d):
        return {"vocab": z * 8 + lax.rem(x + d, 4) * 2 + yl}

    zy = z * 2 + yl

    def vocab_of(e):
        return {"vocab": lax.div(e, 2) * 8 + x * 2 + lax.rem(e, 2)}

    def at_zy(d):
        return vocab_of(lax.rem(zy + d, 16))

    xy = x * 2 + yl

    def at_xy(d):
        return {"vocab": z * 8 + lax.rem(xy + d, 8)}

    at_y = {"vocab": z * 8 + x * 2 + (1 - yl)}

    barrier = pltpu.get_barrier_semaphore()
    for d in range(1, 16):
        pl.semaphore_signal(barrier, inc=1, device_id=at_zy(d), device_id_type=MESH)
    for d in range(1, 8):
        pl.semaphore_signal(barrier, inc=1, device_id=at_xy(d), device_id_type=MESH)
    for d in range(1, 8):
        o = lax.rem(b + d, 8)
        pl.semaphore_signal(
            barrier, inc=1, device_id={"section": lax.div(o, 4), "tok": lax.rem(o, 4)}, device_id_type=MESH
        )
    own_t = rows_ref[0].astype(F32)
    ga[z, x, yl] = jnp.concatenate([own_t, jnp.zeros((CP - C, T), F32)], axis=0).astype(BF)
    pl.semaphore_wait(barrier, 29)

    def gather_y(g, ss, rs):
        rcopy(g.at[z, x, yl], g.at[z, x, yl], ss.at[0], rs.at[0], at_y)
        await_bytes(g.at[z, x, 1 - yl], rs.at[0])

    def gather(g, ss, rs):
        for d in (4, 3, 5, 2, 6, 1, 7):
            rcopy(g.at[z, x], g.at[z, x], ss.at[1], rs.at[1], at_z(d))
        await_bytes(g.at[pl.ds(0, 7), x], rs.at[1])
        xl = lax.rem(x + 3, 4)
        xr = lax.rem(x + 1, 4)
        rcopy(g.at[:, x], g.at[:, x], ss.at[2], rs.at[2], at_x(1))
        rcopy(g.at[:, x], g.at[:, x], ss.at[2], rs.at[3], at_x(3))
        await_bytes(g.at[:, xl], rs.at[2])
        lo = pl.ds(0, 4)
        hi = pl.ds(4, 4)
        rcopy(g.at[lo, xl], g.at[lo, xl], ss.at[2], rs.at[4], at_x(1))
        await_bytes(g.at[:, xr], rs.at[3])
        rcopy(g.at[hi, xr], g.at[hi, xr], ss.at[2], rs.at[5], at_x(3))
        await_bytes(g.at[lo, x], rs.at[4])
        await_bytes(g.at[hi, x], rs.at[5])

    def gather_sent(g, ss):
        await_bytes(g.at[z, x, yl], ss.at[0])
        await_bytes(g.at[pl.ds(0, 7), x], ss.at[1])
        await_bytes(g.at[:, pl.ds(0, 3)], ss.at[2])

    def ring_start(own, piece, ss, rs):
        right = {"tok": t_right}
        left = {"tok": t_left}
        rcopy(own(0), piece(b, 0), ss, rs.at[0], right)
        rcopy(own(1), piece(b, 1), ss, rs.at[3], left)
        rcopy(own(0), piece(b, 0), ss, rs.at[6], sib)
        rcopy(own(1), piece(b, 1), ss, rs.at[6], sib)
        rcopy(own(1), piece(b, 1), ss, rs.at[1], right)
        rcopy(own(0), piece(b, 0), ss, rs.at[2], left)

    def hand(piece, blk, h, ss, rs):
        rcopy(piece(blk, h), piece(blk, h), ss, rs.at[6], sib)

    def ring_mid(piece, ss, rs):
        bl = s * 4 + t_left
        br = s * 4 + t_right
        await_bytes(piece(bl, 0), rs.at[0])
        rcopy(piece(bl, 0), piece(bl, 0), ss, rs.at[4], {"tok": t_right})
        await_bytes(piece(br, 1), rs.at[3])
        rcopy(piece(br, 1), piece(br, 1), ss, rs.at[5], {"tok": t_left})
        hand(piece, bl, 0, ss, rs)
        hand(piece, br, 1, ss, rs)

    def ring_late(piece, ss, rs):
        bl = s * 4 + t_left
        br = s * 4 + t_right
        bf = s * 4 + t_far
        await_bytes(piece(bl, 1), rs.at[1])
        hand(piece, bl, 1, ss, rs)
        await_bytes(piece(br, 0), rs.at[2])
        hand(piece, br, 0, ss, rs)
        await_bytes(piece(bf, 0), rs.at[4])
        hand(piece, bf, 0, ss, rs)
        await_bytes(piece(bf, 1), rs.at[5])
        hand(piece, bf, 1, ss, rs)

    def w_own(h):
        return w_ref.at[pl.ds(224 * h, 224), :]

    def w_piece(blk, h):
        return wf.at[pl.ds(pl.multiple_of(KB * blk + 224 * h, 32), 224), :]

    def l_piece(blk, h):
        return lg_all.at[pl.ds(512 * h, 512), pl.ds(pl.multiple_of(blk * T, T), T)]

    def l_own(h):
        return l_piece(b, h)

    pcopy = pltpu.make_async_copy(proj_ref, proj, loc_sem.at[0])
    pcopy.start()
    gather_y(ga, g1s, g1r)
    ring_start(w_own, w_piece, w_s, w_r)
    wcopy = pltpu.make_async_copy(w_ref, wf.at[pl.ds(pl.multiple_of(KB * b, 64), KB), :], loc_sem.at[1])
    wcopy.start()

    def normalize(g):
        def add(i, acc):
            for j in range(8):
                blk = g[i, j // 2, j % 2][:C, :].astype(F32)
                acc = acc + (blk * blk)
            return acc

        total = lax.fori_loop(0, 8, add, jnp.zeros((C, T), F32))
        inv = lax.rsqrt(jnp.sum(total, axis=0, keepdims=True) * (1.0 / D) + EPS)

        def scale(i, carry):
            parts = [g[i, j // 2, j % 2][:C, :].astype(F32) for j in range(8)]
            block = jnp.concatenate(parts, axis=0) * inv
            r = pl.multiple_of(i * KB, KB)
            normed[pl.ds(r, KB), :] = block
            rt[pl.ds(r, KB), :] = block.astype(BF)
            return carry

        lax.fori_loop(0, 8, scale, 0)
        return inv

    pcopy.wait()

    @pl.when(s == 1)
    def _():
        odd = lax.rem(z, 2) == 1

        def turn_proj(i, carry):
            r = pl.multiple_of(i * T, T)
            block = proj[:, pl.ds(r, T)].astype(F32)
            even_place = jnp.concatenate([block, jnp.zeros((T - C, T), F32)], axis=0)
            odd_place = jnp.concatenate([jnp.zeros((CP, T), F32), block, jnp.zeros((CP - C, T), F32)], axis=0)
            ph[pl.ds(r, T), :] = jnp.where(odd, odd_place, even_place).T.astype(BF)
            return carry

        lax.fori_loop(0, D // T, turn_proj, 0)
        for d in (4, 3, 5, 2, 6, 1, 7):
            zo = lax.rem(z + d, 8)
            rcopy(ph.at[pl.ds(pl.multiple_of(zo * KB, 64), KB), :], phr.at[z], p_s, p_r, at_z(d))
        phr[z] = ph[pl.ds(pl.multiple_of(z * KB, 64), KB), :]

    gather(ga, g1s, g1r)
    inv1 = normalize(ga)
    part = jnp.dot(proj[:, pl.ds(pl.multiple_of(s * D, D), D)], rt[...], preferred_element_type=F32)
    own_rows = pl.ds(pl.multiple_of(v * C, 8), C)

    @pl.when(s == 0)
    def _():
        xch[pl.ds(0, C), :] = part
        xch[pl.ds(C, 8), :] = jnp.broadcast_to(inv1, (8, T))
        xch[pl.ds(CP, C), :] = normed[own_rows, :]
        xch[pl.ds(CP + C, 8), :] = jnp.zeros((8, T), F32)
        rcopy(xch, xin, x_s.at[0], x_r.at[0], sib)
        inv_keep[...] = jnp.broadcast_to(inv1, (8, T))
        ring_mid(w_piece, w_s, w_r)

    @pl.when(s == 1)
    def _():
        await_bytes(xin, x_r.at[0])
        mixed = part + xin[pl.ds(0, C), :]
        gb[z, x, yl] = jnp.concatenate([mixed, jnp.zeros((CP - C, T), F32)], axis=0).astype(BF)
        gather_y(gb, g2s, g2r)
        gather(gb, g2s, g2r)
        inv_keep[...] = jnp.broadcast_to(normalize(gb), (8, T))
        ring_mid(w_piece, w_s, w_r)
        await_bytes(phr.at[pl.ds(0, 7)], p_r)
        for i in range(4):
            pb[:, pl.ds(i * T, T)] = phr[2 * i] + phr[2 * i + 1]

    def turn(i, carry):
        r = pl.multiple_of(i * T, T)
        rnd[:, pl.ds(r, T)] = normed[pl.ds(r, T), :].T.astype(BF)
        return carry

    lax.fori_loop(0, D // T, turn, 0)
    ring_late(w_piece, w_s, w_r)
    wcopy.wait()
    await_bytes(wf.at[pl.ds(0, 4 * KB), :], w_r.at[6])

    def to_owner(d, carry):
        o = lax.rem(b + d, 8)
        rcopy(
            rt.at[pl.ds(pl.multiple_of(o * KB, 64), KB), :],
            r_all.at[:, pl.ds(pl.multiple_of(b * T, T), T)],
            r_s, r_r, {"section": lax.div(o, 4), "tok": lax.rem(o, 4)},
        )
        return carry

    def logits_tile(i, carry):
        r = pl.multiple_of(i * 256, 256)
        tile = jnp.dot(rnd[...], wf[:, pl.ds(r, 256)], preferred_element_type=F32)
        logt[pl.ds(r, 256), :] = tile.T
        return carry

    lax.fori_loop(0, 4, logits_tile, 0)
    r_all[:, pl.ds(pl.multiple_of(b * T, T), T)] = rt[pl.ds(pl.multiple_of(b * KB, 64), KB), :]

    label = lab_ref[...] - v * VS
    place = lax.broadcasted_iota(jnp.int32, (VS, T), 0)
    hit = place == label
    values = logt[...]
    top = jnp.max(values, axis=0, keepdims=True)
    expo = jnp.exp(values - top)
    den = jnp.sum(expo, axis=0, keepdims=True)
    sel = jnp.sum(expo * values, axis=0, keepdims=True)
    lab = jnp.sum(jnp.where(hit, values, 0.0), axis=0, keepdims=True)

    def combine(slots):
        m = slots[0][0:1]
        for q in slots[1:]:
            m = jnp.maximum(m, q[0:1])
        d_ = jnp.zeros((1, T), F32)
        e_ = jnp.zeros((1, T), F32)
        l_ = jnp.zeros((1, T), F32)
        for q in slots:
            f = jnp.exp(q[0:1] - m)
            d_ = d_ + q[1:2] * f
            e_ = e_ + q[2:3] * f
            l_ = l_ + q[3:4]
        return jnp.concatenate([m, d_, e_, l_, jnp.zeros((4, T), F32)], axis=0)

    sx[xy] = jnp.concatenate([top, den, sel, lab, jnp.zeros((4, T), F32)], axis=0)
    for d in (4, 5, 3, 1, 7, 2, 6):
        rcopy(sx.at[xy], sx.at[xy], st_s.at[0], st_r.at[0], at_xy(d))
    lax.fori_loop(1, 8, to_owner, 0)
    await_bytes(sx.at[pl.ds(0, 7)], st_r.at[0])
    sz[z] = combine([sx[i] for i in range(8)])
    for d in (4, 3, 5, 2, 6, 1, 7):
        rcopy(sz.at[z], sz.at[z], st_s.at[1], st_r.at[1], at_z(d))
    await_bytes(sz.at[pl.ds(0, 7)], st_r.at[1])
    stats = combine([sz[i] for i in range(8)])
    weighting = jnp.where(s == 1, MTP_WEIGHT, 1.0).astype(F32)
    inv_den = 1.0 / stats[1:2]
    mean_dot = weighting * (stats[2:3] * inv_den - stats[3:4]) * (1.0 / D)
    prob = jnp.exp(logt[...] - stats[0:1]) * inv_den
    lgt = (weighting * (prob - hit.astype(F32))).astype(BF)
    lg_all[:, pl.ds(pl.multiple_of(b * T, T), T)] = lgt

    pad = jnp.zeros((CP - C, T), F32)

    def spread(block, p, i):
        for j in range(8):
            p[i, j // 2, j % 2] = jnp.concatenate([block[C * j:C * (j + 1), :], pad], axis=0).astype(BF)

    def group(d):
        return lax.rem(lax.div(z, GROUP) + d, GROUPS)

    def blocks(d):
        return pl.ds(pl.multiple_of(group(d) * GROUP, GROUP), GROUP)

    def scatter_x(make, p, rx, ss, rs):
        for n in range(GROUPS):
            d = GROUPS - 1 - n
            for k in range(GROUP):
                make(group(d) * GROUP + k)
            for dx in (2, 1, 3):
                xo = lax.rem(x + dx, 4)
                rcopy(p.at[blocks(d), xo], rx.at[x, blocks(d)], ss, rs.at[d], at_x(dx))

    def scatter_zy(p, rx, az, af, rz, ss, rs, ss2, rs2):
        for n in range(GROUPS):
            d = GROUPS - 1 - n
            await_bytes(rx.at[pl.ds(0, 3), blocks(d)], rs.at[d])
            for k in range(GROUP):
                i = group(d) * GROUP + k
                for j in range(2):
                    a = p[i, x, j].astype(F32)
                    for dx in range(1, 4):
                        a = a + rx[lax.rem(x + dx, 4), i, j].astype(F32)
                    e = i * 2 + j
                    af[e] = a
                    az[e] = a.astype(BF)

                    @pl.when(e != zy)
                    def _():
                        rcopy(az.at[e], rz.at[zy], ss2, rs2, vocab_of(e))
        ring_start(l_own, l_piece, l_s, l_r)
        await_bytes(rz.at[pl.ds(0, 15)], rs2)
        a = af[zy]
        for d in range(1, 16):
            a = a + rz[lax.rem(zy + d, 16)].astype(F32)
        return a[:C, :]

    def scatter_sent(rx, rz, ss, ss2):
        await_bytes(rx.at[pl.ds(0, 3)], ss)
        await_bytes(rz.at[pl.ds(0, 15)], ss2)

    def feature(i):
        block = jnp.dot(wf[pl.ds(pl.multiple_of(i * KB, KB), KB), :], lgt, preferred_element_type=F32)
        spread(block, p3, i)

    scatter_x(feature, p3, rx3, q3s.at[0], q3r)
    fgrad = scatter_zy(p3, rx3, az3, af3, rz3, q3s.at[0], q3r, q3s.at[1], q3r.at[8])
    back = (fgrad - normed[own_rows, :] * mean_dot) * inv_keep[0:1]

    def head_grad():
        await_bytes(r_all.at[:, pl.ds(0, 7 * T)], r_r)
        ring_late(l_piece, l_s, l_r)
        await_bytes(lg_all.at[:, pl.ds(0, 4 * T)], l_r.at[6])

        def tile(i, carry):
            r = pl.multiple_of(i * 256, 256)
            g = lax.dot_general(
                r_all[...], lg_all[pl.ds(r, 256), :], (((1,), (1,)), ((), ())), preferred_element_type=F32
            )
            hg_ref[:, pl.ds(r, 256)] = g.astype(BF)
            return carry

        lax.fori_loop(0, 4, tile, 0)

    @pl.when(s == 0)
    def _():
        bk[...] = back
        rcopy(bk, bkin, x_s.at[1], x_r.at[1], sib)
        ring_mid(l_piece, l_s, l_r)
        head_grad()
        await_bytes(bkin, x_r.at[1])
        out_ref[...] = back + bkin[...]
        await_bytes(xch, x_s.at[0])

    @pl.when(s == 1)
    def _():
        mg = back.astype(BF)
        hdot = jnp.sum(mg.astype(F32) * xin[pl.ds(0, C), :], axis=0, keepdims=True)
        high = hdot.astype(BF).astype(F32)
        middle = (hdot - high).astype(BF).astype(F32)
        low = hdot - high - middle
        mgb[z] = jnp.concatenate(
            [mg.astype(F32), high, middle, low, jnp.zeros((5, T), F32)], axis=0
        ).astype(BF)
        for d in (4, 3, 5, 2, 6, 1, 7):
            rcopy(mgb.at[z], mgb.at[z], m_s, m_r, at_z(d))
        await_bytes(mgb.at[pl.ds(0, 7)], m_r)
        hsum = jnp.zeros((8, T), F32)
        for i in range(8):
            hsum = hsum + mgb[i, pl.ds(C - 8, 16), :].astype(F32)[8:16]
        hrow = hsum[0:1] + hsum[1:2] + hsum[2:3]
        joint = jnp.dot(pb[...], mgb[...].reshape(8 * CP, T), preferred_element_type=F32)
        for j in range(8):
            jb[j] = jnp.concatenate([joint[C * j:C * (j + 1), :], jnp.broadcast_to(hrow, (8, T))], axis=0)
        for d in (4, 5, 3, 1, 7, 2, 6):
            rcopy(jb.at[lax.rem(xy + d, 8)], jx.at[xy], j_s, j_r, at_xy(d))
        ring_mid(l_piece, l_s, l_r)
        await_bytes(jx.at[pl.ds(0, 7)], j_r)
        tot = jb[xy]
        for d in range(1, 8):
            tot = tot + jx[lax.rem(xy + d, 8)]
        jgrad = tot[:C, :]
        hmean = tot[C:C + 1] * (1.0 / D)
        depth = (jgrad - xin[pl.ds(CP, C), :] * hmean) * xin[pl.ds(C, 1), :]
        bk[...] = depth
        rcopy(bk, bkin, x_s.at[1], x_r.at[1], sib)
        await_bytes(bkin, x_r.at[1])
        out_ref[...] = bkin[...] + depth
        head_grad()
        gather_sent(gb, g2s)
        await_bytes(mgb.at[pl.ds(0, 7)], m_s)
        await_bytes(jx.at[pl.ds(0, 7)], j_s)
        await_bytes(phr.at[pl.ds(0, 7)], p_s)

    await_bytes(bk, x_s.at[1])
    gather_sent(ga, g1s)
    scatter_sent(rx3, rz3, q3s.at[0], q3s.at[1])
    await_bytes(sx.at[pl.ds(0, 7)], st_s.at[0])
    await_bytes(sz.at[pl.ds(0, 7)], st_s.at[1])
    await_bytes(r_all.at[:, pl.ds(0, 7 * T)], r_s)
    await_bytes(wf.at[pl.ds(0, 7 * KB), :], w_s)
    await_bytes(lg_all.at[:, pl.ds(0, 7 * T)], l_s)


def local(rows, targets, proj_weight, head_weight):
    vm = pl.BlockSpec(memory_space=pltpu.VMEM)
    anyspace = pl.BlockSpec(memory_space=pl.ANY)
    dma = pltpu.SemaphoreType.DMA

    def rs_bufs():
        return [
            pltpu.VMEM((8, 4, 2, CP, T), BF),
            pltpu.VMEM((4, 8, 2, CP, T), BF),
            pltpu.VMEM((16, CP, T), BF),
            pltpu.VMEM((16, CP, T), F32),
            pltpu.VMEM((16, CP, T), BF),
        ]

    head_grad, grad_t = pl.pallas_call(
        kernel,
        out_shape=(
            jax.ShapeDtypeStruct((KB, VS), BF),
            jax.ShapeDtypeStruct((C, T), F32),
        ),
        in_specs=[vm, vm, anyspace, anyspace],
        out_specs=(vm, vm),
        scratch_shapes=[
            pltpu.VMEM((D, VS), BF),
            pltpu.VMEM((C, 2 * D), BF),
            pltpu.VMEM((D, T), BF),
            pltpu.VMEM((8, 4, 2, CP, T), BF),
            pltpu.VMEM((8, 4, 2, CP, T), BF),
            pltpu.VMEM((D, T), F32),
            pltpu.VMEM((D, T), BF),
            pltpu.VMEM((T, D), BF),
            pltpu.VMEM((VS, T), F32),
            pltpu.VMEM((VS, 8 * T), BF),
            pltpu.VMEM((KB, 8 * T), BF),
            *rs_bufs(),
            pltpu.VMEM((8, KB, T), BF),
            pltpu.VMEM((KB, 8 * CP), BF),
            pltpu.VMEM((8, CP, T), BF),
            pltpu.VMEM((8, CP, T), F32),
            pltpu.VMEM((8, CP, T), F32),
            pltpu.VMEM((8, 8, T), F32),
            pltpu.VMEM((8, 8, T), F32),
            pltpu.VMEM((8, T), F32),
            pltpu.VMEM((2 * CP, T), F32),
            pltpu.VMEM((2 * CP, T), F32),
            pltpu.VMEM((C, T), F32),
            pltpu.VMEM((C, T), F32),
            dma((2,)), dma, dma((7,)), dma, dma((7,)), dma, dma,
            dma((3,)), dma((6,)), dma((3,)), dma((6,)),
            dma((2,)), dma((2,)), dma((2,)), dma((9,)),
            dma, dma, dma, dma, dma, dma,
            dma((2,)), dma((2,)),
        ],
        compiler_params=pltpu.CompilerParams(
            collective_id=0, has_side_effects=True, vmem_limit_bytes=56 * 1024 * 1024
        ),
        cost_estimate=pl.CostEstimate(flops=3 * 10**9, bytes_accessed=2 * 10**7, transcendentals=3 * 10**5),
        name="head",
    )(jnp.swapaxes(rows, 1, 2), targets, proj_weight.T, head_weight)
    return head_grad, grad_t.T


def solution(mesh):
    placed = (
        P("section", "tok", "vocab"),
        P("section", "tok"),
        P(None, "vocab"),
        P(("section", "tok"), "vocab"),
    )
    return jax.shard_map(
        local,
        mesh=mesh,
        in_specs=placed,
        out_specs=(P(("section", "tok"), "vocab"), P("tok", "vocab")),
        check_vma=False,
    )
```

```python
import jax
import jax.numpy as jnp
from jax import lax
from jax.experimental import pallas as pl
from jax.experimental.pallas import tpu as pltpu
from jax.sharding import PartitionSpec as P

EPS = 1e-06
MTP_WEIGHT = 0.3
D = 3584
T = 128
C = 56
CP = 64
VS = 1024
KB = 448
SHARE = KB // 4
MESH = pl.DeviceIdType.MESH
ORDER = (8, 7, 9, 6, 10, 5, 11, 4, 12, 3, 13, 2, 14, 1, 15)
GROUP = 2
GROUPS = 8 // GROUP
BF = jnp.bfloat16
F32 = jnp.float32


def rcopy(src, dst, ssem, rsem, dev):
    copy = pltpu.make_async_remote_copy(
        src_ref=src, dst_ref=dst, send_sem=ssem, recv_sem=rsem, device_id=dev, device_id_type=MESH
    )
    copy.start()


def await_bytes(ref, sem):
    pltpu.make_async_copy(ref, ref, sem).wait()


def kernel(
    rows_ref, lab_ref, proj_ref, w_ref, hg_ref, out_ref,
    wf, proj, ph, ga, gb, normed, rt, rnd, logt, lg_all, r_all,
    p3, rx3, az3, af3, rz3,
    phr, pb, mgb, jb, jx, sx, sz, inv_keep,
    xch, xin, bk, bkin,
    loc_sem, w_s, w_r, l_s, l_r, r_s, r_r,
    g1s, g1r, g2s, g2r, st_s, st_r, q3s, q3r, p_s, p_r, m_s, m_r, j_s, j_r, ra_s, ra_r, x_s, x_r,
):
    s = lax.axis_index("section")
    v = lax.axis_index("vocab")
    t = lax.axis_index("tok")
    z = lax.div(v, 8)
    x = lax.rem(lax.div(v, 2), 4)
    yl = lax.rem(v, 2)
    b = s * 4 + t
    sib = {"section": 1 - s}
    t_right = lax.rem(t + 1, 4)
    t_left = lax.rem(t + 3, 4)
    t_far = lax.rem(t + 2, 4)

    def at_z(d):
        return {"vocab": lax.rem(z + d, 8) * 8 + x * 2 + yl}

    def at_x(d):
        return {"vocab": z * 8 + lax.rem(x + d, 4) * 2 + yl}

    zy = z * 2 + yl

    def vocab_of(e):
        return {"vocab": lax.div(e, 2) * 8 + x * 2 + lax.rem(e, 2)}

    def at_zy(d):
        return vocab_of(lax.rem(zy + d, 16))

    xy = x * 2 + yl

    def at_xy(d):
        return {"vocab": z * 8 + lax.rem(xy + d, 8)}

    at_y = {"vocab": z * 8 + x * 2 + (1 - yl)}

    barrier = pltpu.get_barrier_semaphore()
    for d in range(1, 16):
        pl.semaphore_signal(barrier, inc=1, device_id=at_zy(d), device_id_type=MESH)
    for d in range(1, 8):
        pl.semaphore_signal(barrier, inc=1, device_id=at_xy(d), device_id_type=MESH)
    for d in range(1, 8):
        o = lax.rem(b + d, 8)
        pl.semaphore_signal(
            barrier, inc=1, device_id={"section": lax.div(o, 4), "tok": lax.rem(o, 4)}, device_id_type=MESH
        )
    own_t = rows_ref[0].astype(F32)
    ga[z, x, yl] = jnp.concatenate([own_t, jnp.zeros((CP - C, T), F32)], axis=0).astype(BF)
    pl.semaphore_wait(barrier, 29)

    def gather_y(g, ss, rs):
        rcopy(g.at[z, x, yl], g.at[z, x, yl], ss.at[0], rs.at[0], at_y)
        await_bytes(g.at[z, x, 1 - yl], rs.at[0])

    def gather(g, ss, rs):
        for d in (4, 3, 5, 2, 6, 1, 7):
            rcopy(g.at[z, x], g.at[z, x], ss.at[1], rs.at[1], at_z(d))
        await_bytes(g.at[pl.ds(0, 7), x], rs.at[1])
        xl = lax.rem(x + 3, 4)
        xr = lax.rem(x + 1, 4)
        rcopy(g.at[:, x], g.at[:, x], ss.at[2], rs.at[2], at_x(1))
        rcopy(g.at[:, x], g.at[:, x], ss.at[2], rs.at[3], at_x(3))
        await_bytes(g.at[:, xl], rs.at[2])
        lo = pl.ds(0, 4)
        hi = pl.ds(4, 4)
        rcopy(g.at[lo, xl], g.at[lo, xl], ss.at[2], rs.at[4], at_x(1))
        await_bytes(g.at[:, xr], rs.at[3])
        rcopy(g.at[hi, xr], g.at[hi, xr], ss.at[2], rs.at[5], at_x(3))
        await_bytes(g.at[lo, x], rs.at[4])
        await_bytes(g.at[hi, x], rs.at[5])

    def gather_sent(g, ss):
        await_bytes(g.at[z, x, yl], ss.at[0])
        await_bytes(g.at[pl.ds(0, 7), x], ss.at[1])
        await_bytes(g.at[:, pl.ds(0, 3)], ss.at[2])

    def ring_start(own, piece, ss, rs):
        right = {"tok": t_right}
        left = {"tok": t_left}
        rcopy(own(0), piece(b, 0), ss, rs.at[0], right)
        rcopy(own(1), piece(b, 1), ss, rs.at[3], left)

    def ring_second(own, piece, ss, rs):
        right = {"tok": t_right}
        left = {"tok": t_left}
        rcopy(own(0), piece(b, 0), ss, rs.at[6], sib)
        rcopy(own(1), piece(b, 1), ss, rs.at[6], sib)
        rcopy(own(1), piece(b, 1), ss, rs.at[1], right)
        rcopy(own(0), piece(b, 0), ss, rs.at[2], left)

    def hand(piece, blk, h, ss, rs):
        rcopy(piece(blk, h), piece(blk, h), ss, rs.at[6], sib)

    def ring_mid(piece, ss, rs):
        bl = s * 4 + t_left
        br = s * 4 + t_right
        await_bytes(piece(bl, 0), rs.at[0])
        rcopy(piece(bl, 0), piece(bl, 0), ss, rs.at[4], {"tok": t_right})
        await_bytes(piece(br, 1), rs.at[3])
        rcopy(piece(br, 1), piece(br, 1), ss, rs.at[5], {"tok": t_left})
        hand(piece, bl, 0, ss, rs)
        hand(piece, br, 1, ss, rs)

    def ring_late(piece, ss, rs):
        bl = s * 4 + t_left
        br = s * 4 + t_right
        bf = s * 4 + t_far
        await_bytes(piece(bl, 1), rs.at[1])
        hand(piece, bl, 1, ss, rs)
        await_bytes(piece(br, 0), rs.at[2])
        hand(piece, br, 0, ss, rs)
        await_bytes(piece(bf, 0), rs.at[4])
        hand(piece, bf, 0, ss, rs)
        await_bytes(piece(bf, 1), rs.at[5])
        hand(piece, bf, 1, ss, rs)

    def w_own(h):
        return w_ref.at[pl.ds(224 * h, 224), :]

    def w_piece(blk, h):
        return wf.at[pl.ds(pl.multiple_of(KB * blk + 224 * h, 32), 224), :]

    def l_piece(blk, h):
        return lg_all.at[pl.ds(512 * h, 512), pl.ds(pl.multiple_of(blk * T, T), T)]

    def l_own(h):
        return l_piece(b, h)

    pcopy = pltpu.make_async_copy(proj_ref, proj, loc_sem.at[0])
    pcopy.start()
    gather_y(ga, g1s, g1r)
    ring_start(w_own, w_piece, w_s, w_r)
    ring_second(w_own, w_piece, w_s, w_r)
    wcopy = pltpu.make_async_copy(w_ref, wf.at[pl.ds(pl.multiple_of(KB * b, 64), KB), :], loc_sem.at[1])
    wcopy.start()

    def normalize(g):
        def add(i, acc):
            for j in range(8):
                blk = g[i, j // 2, j % 2][:C, :].astype(F32)
                acc = acc + (blk * blk)
            return acc

        total = lax.fori_loop(0, 8, add, jnp.zeros((C, T), F32))
        inv = lax.rsqrt(jnp.sum(total, axis=0, keepdims=True) * (1.0 / D) + EPS)

        def scale(i, carry):
            parts = [g[i, j // 2, j % 2][:C, :].astype(F32) for j in range(8)]
            block = jnp.concatenate(parts, axis=0) * inv
            r = pl.multiple_of(i * KB, KB)
            normed[pl.ds(r, KB), :] = block
            rt[pl.ds(r, KB), :] = block.astype(BF)
            return carry

        lax.fori_loop(0, 8, scale, 0)
        return inv

    pcopy.wait()

    @pl.when(s == 1)
    def _():
        odd = lax.rem(z, 2) == 1

        def turn_proj(i, carry):
            r = pl.multiple_of(i * T, T)
            block = proj[:, pl.ds(r, T)].astype(F32)
            even_place = jnp.concatenate([block, jnp.zeros((T - C, T), F32)], axis=0)
            odd_place = jnp.concatenate([jnp.zeros((CP, T), F32), block, jnp.zeros((CP - C, T), F32)], axis=0)
            ph[pl.ds(r, T), :] = jnp.where(odd, odd_place, even_place).T.astype(BF)
            return carry

        lax.fori_loop(0, D // T, turn_proj, 0)
        for d in (4, 3, 5, 2, 6, 1, 7):
            zo = lax.rem(z + d, 8)
            rcopy(ph.at[pl.ds(pl.multiple_of(zo * KB, 64), KB), :], phr.at[z], p_s, p_r, at_z(d))
        phr[z] = ph[pl.ds(pl.multiple_of(z * KB, 64), KB), :]

    gather(ga, g1s, g1r)
    inv1 = normalize(ga)
    part = jnp.dot(proj[:, pl.ds(pl.multiple_of(s * D, D), D)], rt[...], preferred_element_type=F32)
    own_rows = pl.ds(pl.multiple_of(v * C, 8), C)

    @pl.when(s == 0)
    def _():
        xch[pl.ds(0, C), :] = part
        xch[pl.ds(C, 8), :] = jnp.broadcast_to(inv1, (8, T))
        xch[pl.ds(CP, C), :] = normed[own_rows, :]
        xch[pl.ds(CP + C, 8), :] = jnp.zeros((8, T), F32)
        rcopy(xch, xin, x_s.at[0], x_r.at[0], sib)
        inv_keep[...] = jnp.broadcast_to(inv1, (8, T))
        ring_mid(w_piece, w_s, w_r)

    @pl.when(s == 1)
    def _():
        await_bytes(xin, x_r.at[0])
        mixed = part + xin[pl.ds(0, C), :]
        gb[z, x, yl] = jnp.concatenate([mixed, jnp.zeros((CP - C, T), F32)], axis=0).astype(BF)
        rcopy(gb.at[z, x, yl], gb.at[z, x, yl], g2s.at[0], g2r.at[0], at_y)
        ring_mid(w_piece, w_s, w_r)
        await_bytes(gb.at[z, x, 1 - yl], g2r.at[0])
        gather(gb, g2s, g2r)
        inv_keep[...] = jnp.broadcast_to(normalize(gb), (8, T))
        await_bytes(phr.at[pl.ds(0, 7)], p_r)
        for i in range(4):
            pb[:, pl.ds(i * T, T)] = phr[2 * i] + phr[2 * i + 1]

    def turn(i, carry):
        r = pl.multiple_of(i * T, T)
        rnd[:, pl.ds(r, T)] = normed[pl.ds(r, T), :].T.astype(BF)
        return carry

    lax.fori_loop(0, D // T, turn, 0)
    ring_late(w_piece, w_s, w_r)
    wcopy.wait()
    await_bytes(wf.at[pl.ds(0, 4 * KB), :], w_r.at[6])

    part_rows = pl.ds(pl.multiple_of(x * SHARE, 16), SHARE)
    own_tokens = pl.ds(pl.multiple_of(b * T, T), T)

    def rows_of(o):
        return pl.ds(pl.multiple_of(o * KB + x * SHARE, 16), SHARE)

    def to_owner(d, carry):
        o = lax.rem(b + d, 8)
        rcopy(
            rt.at[rows_of(o), :], r_all.at[part_rows, own_tokens],
            r_s, r_r, {"section": lax.div(o, 4), "tok": lax.rem(o, 4)},
        )
        return carry

    def share_rows():
        await_bytes(r_all.at[part_rows, pl.ds(0, 7 * T)], r_r)
        for d in (2, 1, 3):
            rcopy(r_all.at[part_rows, :], r_all.at[part_rows, :], ra_s, ra_r, at_x(d))

    def logits_tile(i, carry):
        r = pl.multiple_of(i * 256, 256)
        tile = jnp.dot(rnd[...], wf[:, pl.ds(r, 256)], preferred_element_type=F32)
        logt[pl.ds(r, 256), :] = tile.T
        return carry

    lax.fori_loop(0, 4, logits_tile, 0)
    r_all[part_rows, own_tokens] = rt[rows_of(b), :]

    label = lab_ref[...] - v * VS
    place = lax.broadcasted_iota(jnp.int32, (VS, T), 0)
    hit = place == label
    values = logt[...]
    top = jnp.max(values, axis=0, keepdims=True)
    expo = jnp.exp(values - top)
    den = jnp.sum(expo, axis=0, keepdims=True)
    sel = jnp.sum(expo * values, axis=0, keepdims=True)
    lab = jnp.sum(jnp.where(hit, values, 0.0), axis=0, keepdims=True)

    def combine(slots):
        m = slots[0][0:1]
        for q in slots[1:]:
            m = jnp.maximum(m, q[0:1])
        d_ = jnp.zeros((1, T), F32)
        e_ = jnp.zeros((1, T), F32)
        l_ = jnp.zeros((1, T), F32)
        for q in slots:
            f = jnp.exp(q[0:1] - m)
            d_ = d_ + q[1:2] * f
            e_ = e_ + q[2:3] * f
            l_ = l_ + q[3:4]
        return jnp.concatenate([m, d_, e_, l_, jnp.zeros((4, T), F32)], axis=0)

    sx[xy] = jnp.concatenate([top, den, sel, lab, jnp.zeros((4, T), F32)], axis=0)
    for d in (4, 5, 3, 1, 7, 2, 6):
        rcopy(sx.at[xy], sx.at[xy], st_s.at[0], st_r.at[0], at_xy(d))
    lax.fori_loop(1, 8, to_owner, 0)
    await_bytes(sx.at[pl.ds(0, 7)], st_r.at[0])
    sz[z] = combine([sx[i] for i in range(8)])
    for d in (4, 3, 5, 2, 6, 1, 7):
        rcopy(sz.at[z], sz.at[z], st_s.at[1], st_r.at[1], at_z(d))
    await_bytes(sz.at[pl.ds(0, 7)], st_r.at[1])
    stats = combine([sz[i] for i in range(8)])
    weighting = jnp.where(s == 1, MTP_WEIGHT, 1.0).astype(F32)
    inv_den = 1.0 / stats[1:2]
    mean_dot = weighting * (stats[2:3] * inv_den - stats[3:4]) * (1.0 / D)
    prob = jnp.exp(logt[...] - stats[0:1]) * inv_den
    lgt = (weighting * (prob - hit.astype(F32))).astype(BF)
    lg_all[:, pl.ds(pl.multiple_of(b * T, T), T)] = lgt

    ring_start(l_own, l_piece, l_s, l_r)
    pad = jnp.zeros((CP - C, T), F32)

    def spread(block, p, i):
        for j in range(8):
            p[i, j // 2, j % 2] = jnp.concatenate([block[C * j:C * (j + 1), :], pad], axis=0).astype(BF)

    def group(d):
        return lax.rem(lax.div(z, GROUP) + d, GROUPS)

    def blocks(d):
        return pl.ds(pl.multiple_of(group(d) * GROUP, GROUP), GROUP)

    def scatter_x(make, p, rx, ss, rs):
        for n in range(GROUPS):
            d = GROUPS - 1 - n
            for k in range(GROUP):
                make(group(d) * GROUP + k)
            for dx in (2, 1, 3):
                xo = lax.rem(x + dx, 4)
                rcopy(p.at[blocks(d), xo], rx.at[x, blocks(d)], ss, rs.at[d], at_x(dx))

    def scatter_zy(p, rx, az, af, rz, ss, rs, ss2, rs2):
        for n in range(GROUPS):
            d = GROUPS - 1 - n
            await_bytes(rx.at[pl.ds(0, 3), blocks(d)], rs.at[d])
            for k in range(GROUP):
                i = group(d) * GROUP + k
                for j in range(2):
                    a = p[i, x, j].astype(F32)
                    for dx in range(1, 4):
                        a = a + rx[lax.rem(x + dx, 4), i, j].astype(F32)
                    e = i * 2 + j
                    af[e] = a
                    az[e] = a.astype(BF)

                    @pl.when(e != zy)
                    def _():
                        rcopy(az.at[e], rz.at[zy], ss2, rs2, vocab_of(e))
        ring_second(l_own, l_piece, l_s, l_r)
        ring_mid(l_piece, l_s, l_r)
        share_rows()
        await_bytes(rz.at[pl.ds(0, 15)], rs2)
        a = af[zy]
        for d in range(1, 16):
            a = a + rz[lax.rem(zy + d, 16)].astype(F32)
        return a[:C, :]

    def scatter_sent(rx, rz, ss, ss2):
        await_bytes(rx.at[pl.ds(0, 3)], ss)
        await_bytes(rz.at[pl.ds(0, 15)], ss2)

    def feature(i):
        block = jnp.dot(wf[pl.ds(pl.multiple_of(i * KB, KB), KB), :], lgt, preferred_element_type=F32)
        spread(block, p3, i)

    scatter_x(feature, p3, rx3, q3s.at[0], q3r)
    fgrad = scatter_zy(p3, rx3, az3, af3, rz3, q3s.at[0], q3r, q3s.at[1], q3r.at[8])
    back = (fgrad - normed[own_rows, :] * mean_dot) * inv_keep[0:1]

    def head_grad():
        await_bytes(r_all.at[pl.ds(0, 3 * SHARE), :], ra_r)
        ring_late(l_piece, l_s, l_r)
        await_bytes(lg_all.at[:, pl.ds(0, 4 * T)], l_r.at[6])

        def tile(i, carry):
            r = pl.multiple_of(i * 256, 256)
            g = lax.dot_general(
                r_all[...], lg_all[pl.ds(r, 256), :], (((1,), (1,)), ((), ())), preferred_element_type=F32
            )
            hg_ref[:, pl.ds(r, 256)] = g.astype(BF)
            return carry

        lax.fori_loop(0, 4, tile, 0)

    @pl.when(s == 0)
    def _():
        bk[...] = back
        rcopy(bk, bkin, x_s.at[1], x_r.at[1], sib)
        head_grad()
        await_bytes(bkin, x_r.at[1])
        out_ref[...] = back + bkin[...]
        await_bytes(xch, x_s.at[0])

    @pl.when(s == 1)
    def _():
        mg = back.astype(BF)
        hdot = jnp.sum(mg.astype(F32) * xin[pl.ds(0, C), :], axis=0, keepdims=True)
        high = hdot.astype(BF).astype(F32)
        middle = (hdot - high).astype(BF).astype(F32)
        low = hdot - high - middle
        mgb[z] = jnp.concatenate(
            [mg.astype(F32), high, middle, low, jnp.zeros((5, T), F32)], axis=0
        ).astype(BF)
        for d in (4, 3, 5, 2, 6, 1, 7):
            rcopy(mgb.at[z], mgb.at[z], m_s, m_r, at_z(d))
        await_bytes(mgb.at[pl.ds(0, 7)], m_r)
        hsum = jnp.zeros((8, T), F32)
        for i in range(8):
            hsum = hsum + mgb[i, pl.ds(C - 8, 16), :].astype(F32)[8:16]
        hrow = hsum[0:1] + hsum[1:2] + hsum[2:3]
        joint = jnp.dot(pb[...], mgb[...].reshape(8 * CP, T), preferred_element_type=F32)
        for j in range(8):
            jb[j] = jnp.concatenate([joint[C * j:C * (j + 1), :], jnp.broadcast_to(hrow, (8, T))], axis=0)
        for d in (4, 5, 3, 1, 7, 2, 6):
            rcopy(jb.at[lax.rem(xy + d, 8)], jx.at[xy], j_s, j_r, at_xy(d))
        await_bytes(jx.at[pl.ds(0, 7)], j_r)
        tot = jb[xy]
        for d in range(1, 8):
            tot = tot + jx[lax.rem(xy + d, 8)]
        jgrad = tot[:C, :]
        hmean = tot[C:C + 1] * (1.0 / D)
        depth = (jgrad - xin[pl.ds(CP, C), :] * hmean) * xin[pl.ds(C, 1), :]
        bk[...] = depth
        rcopy(bk, bkin, x_s.at[1], x_r.at[1], sib)
        await_bytes(bkin, x_r.at[1])
        out_ref[...] = bkin[...] + depth
        head_grad()
        gather_sent(gb, g2s)
        await_bytes(mgb.at[pl.ds(0, 7)], m_s)
        await_bytes(jx.at[pl.ds(0, 7)], j_s)
        await_bytes(phr.at[pl.ds(0, 7)], p_s)

    await_bytes(bk, x_s.at[1])
    gather_sent(ga, g1s)
    scatter_sent(rx3, rz3, q3s.at[0], q3s.at[1])
    await_bytes(sx.at[pl.ds(0, 7)], st_s.at[0])
    await_bytes(sz.at[pl.ds(0, 7)], st_s.at[1])
    await_bytes(r_all.at[part_rows, pl.ds(0, 7 * T)], r_s)
    await_bytes(r_all.at[pl.ds(0, 3 * SHARE), :], ra_s)
    await_bytes(wf.at[pl.ds(0, 7 * KB), :], w_s)
    await_bytes(lg_all.at[:, pl.ds(0, 7 * T)], l_s)


def local(rows, targets, proj_weight, head_weight):
    vm = pl.BlockSpec(memory_space=pltpu.VMEM)
    anyspace = pl.BlockSpec(memory_space=pl.ANY)
    dma = pltpu.SemaphoreType.DMA

    def rs_bufs():
        return [
            pltpu.VMEM((8, 4, 2, CP, T), BF),
            pltpu.VMEM((4, 8, 2, CP, T), BF),
            pltpu.VMEM((16, CP, T), BF),
            pltpu.VMEM((16, CP, T), F32),
            pltpu.VMEM((16, CP, T), BF),
        ]

    head_grad, grad_t = pl.pallas_call(
        kernel,
        out_shape=(
            jax.ShapeDtypeStruct((KB, VS), BF),
            jax.ShapeDtypeStruct((C, T), F32),
        ),
        in_specs=[vm, vm, anyspace, anyspace],
        out_specs=(vm, vm),
        scratch_shapes=[
            pltpu.VMEM((D, VS), BF),
            pltpu.VMEM((C, 2 * D), BF),
            pltpu.VMEM((D, T), BF),
            pltpu.VMEM((8, 4, 2, CP, T), BF),
            pltpu.VMEM((8, 4, 2, CP, T), BF),
            pltpu.VMEM((D, T), F32),
            pltpu.VMEM((D, T), BF),
            pltpu.VMEM((T, D), BF),
            pltpu.VMEM((VS, T), F32),
            pltpu.VMEM((VS, 8 * T), BF),
            pltpu.VMEM((KB, 8 * T), BF),
            *rs_bufs(),
            pltpu.VMEM((8, KB, T), BF),
            pltpu.VMEM((KB, 8 * CP), BF),
            pltpu.VMEM((8, CP, T), BF),
            pltpu.VMEM((8, CP, T), F32),
            pltpu.VMEM((8, CP, T), F32),
            pltpu.VMEM((8, 8, T), F32),
            pltpu.VMEM((8, 8, T), F32),
            pltpu.VMEM((8, T), F32),
            pltpu.VMEM((2 * CP, T), F32),
            pltpu.VMEM((2 * CP, T), F32),
            pltpu.VMEM((C, T), F32),
            pltpu.VMEM((C, T), F32),
            dma((2,)), dma, dma((7,)), dma, dma((7,)), dma, dma,
            dma((3,)), dma((6,)), dma((3,)), dma((6,)),
            dma((2,)), dma((2,)), dma((2,)), dma((9,)),
            dma, dma, dma, dma, dma, dma, dma, dma,
            dma((2,)), dma((2,)),
        ],
        compiler_params=pltpu.CompilerParams(
            collective_id=0, has_side_effects=True, vmem_limit_bytes=56 * 1024 * 1024
        ),
        cost_estimate=pl.CostEstimate(flops=3 * 10**9, bytes_accessed=2 * 10**7, transcendentals=3 * 10**5),
        name="head",
    )(jnp.swapaxes(rows, 1, 2), targets, proj_weight.T, head_weight)
    return head_grad, grad_t.T


def solution(mesh):
    placed = (
        P("section", "tok", "vocab"),
        P("section", "tok"),
        P(None, "vocab"),
        P(("section", "tok"), "vocab"),
    )
    return jax.shard_map(
        local,
        mesh=mesh,
        in_specs=placed,
        out_specs=(P(("section", "tok"), "vocab"), P("tok", "vocab")),
        check_vma=False,
    )
```

```python
import jax
import jax.numpy as jnp
from jax import lax
from jax.experimental import pallas as pl
from jax.experimental.pallas import tpu as pltpu
from jax.sharding import PartitionSpec as P

EPS = 1e-06
MTP_WEIGHT = 0.3
D = 3584
T = 128
C = 56
CP = 64
VS = 1024
KB = 448
SHARE = KB // 4
MESH = pl.DeviceIdType.MESH
ORDER = (8, 7, 9, 6, 10, 5, 11, 4, 12, 3, 13, 2, 14, 1, 15)
GROUP = 1
GROUPS = 8 // GROUP
BF = jnp.bfloat16
F32 = jnp.float32


def rcopy(src, dst, ssem, rsem, dev):
    copy = pltpu.make_async_remote_copy(
        src_ref=src, dst_ref=dst, send_sem=ssem, recv_sem=rsem, device_id=dev, device_id_type=MESH
    )
    copy.start()


def await_bytes(ref, sem):
    pltpu.make_async_copy(ref, ref, sem).wait()


def kernel(
    rows_ref, lab_ref, proj_ref, w_ref, hg_ref, out_ref,
    wf, proj, ph, ga, gb, normed, rt, rnd, logt, lg_all, r_all,
    p3, rx3, az3, af3, rz3,
    phr, pb, mgb, jb, jx, sx, sz, inv_keep,
    xch, xin, bk, bkin,
    loc_sem, w_s, w_r, l_s, l_r, r_s, r_r,
    g1s, g1r, g2s, g2r, st_s, st_r, q3s, q3r, p_s, p_r, m_s, m_r, j_s, j_r, ra_s, ra_r, x_s, x_r,
):
    s = lax.axis_index("section")
    v = lax.axis_index("vocab")
    t = lax.axis_index("tok")
    z = lax.div(v, 8)
    x = lax.rem(lax.div(v, 2), 4)
    yl = lax.rem(v, 2)
    b = s * 4 + t
    sib = {"section": 1 - s}
    t_right = lax.rem(t + 1, 4)
    t_left = lax.rem(t + 3, 4)
    t_far = lax.rem(t + 2, 4)

    def at_z(d):
        return {"vocab": lax.rem(z + d, 8) * 8 + x * 2 + yl}

    def at_x(d):
        return {"vocab": z * 8 + lax.rem(x + d, 4) * 2 + yl}

    zy = z * 2 + yl

    def vocab_of(e):
        return {"vocab": lax.div(e, 2) * 8 + x * 2 + lax.rem(e, 2)}

    def at_zy(d):
        return vocab_of(lax.rem(zy + d, 16))

    xy = x * 2 + yl

    def at_xy(d):
        return {"vocab": z * 8 + lax.rem(xy + d, 8)}

    at_y = {"vocab": z * 8 + x * 2 + (1 - yl)}

    barrier = pltpu.get_barrier_semaphore()
    for d in range(1, 16):
        pl.semaphore_signal(barrier, inc=1, device_id=at_zy(d), device_id_type=MESH)
    for d in range(1, 8):
        pl.semaphore_signal(barrier, inc=1, device_id=at_xy(d), device_id_type=MESH)
    for d in range(1, 8):
        o = lax.rem(b + d, 8)
        pl.semaphore_signal(
            barrier, inc=1, device_id={"section": lax.div(o, 4), "tok": lax.rem(o, 4)}, device_id_type=MESH
        )
    own_t = rows_ref[0].astype(F32)
    ga[z, x, yl] = jnp.concatenate([own_t, jnp.zeros((CP - C, T), F32)], axis=0).astype(BF)
    pl.semaphore_wait(barrier, 29)

    def gather_y(g, ss, rs):
        rcopy(g.at[z, x, yl], g.at[z, x, yl], ss.at[0], rs.at[0], at_y)
        await_bytes(g.at[z, x, 1 - yl], rs.at[0])

    def gather(g, ss, rs, between):
        for d in (4, 3, 5, 2, 6, 1, 7):
            rcopy(g.at[z, x], g.at[z, x], ss.at[1], rs.at[1], at_z(d))
        between()
        await_bytes(g.at[pl.ds(0, 7), x], rs.at[1])
        xl = lax.rem(x + 3, 4)
        xr = lax.rem(x + 1, 4)
        rcopy(g.at[:, x], g.at[:, x], ss.at[2], rs.at[2], at_x(1))
        rcopy(g.at[:, x], g.at[:, x], ss.at[2], rs.at[3], at_x(3))
        await_bytes(g.at[:, xl], rs.at[2])
        lo = pl.ds(0, 4)
        hi = pl.ds(4, 4)
        rcopy(g.at[lo, xl], g.at[lo, xl], ss.at[2], rs.at[4], at_x(1))
        await_bytes(g.at[:, xr], rs.at[3])
        rcopy(g.at[hi, xr], g.at[hi, xr], ss.at[2], rs.at[5], at_x(3))
        await_bytes(g.at[lo, x], rs.at[4])
        await_bytes(g.at[hi, x], rs.at[5])

    def gather_sent(g, ss):
        await_bytes(g.at[z, x, yl], ss.at[0])
        await_bytes(g.at[pl.ds(0, 7), x], ss.at[1])
        await_bytes(g.at[:, pl.ds(0, 3)], ss.at[2])

    def ring_start(own, piece, ss, rs):
        right = {"tok": t_right}
        left = {"tok": t_left}
        rcopy(own(0), piece(b, 0), ss, rs.at[0], right)
        rcopy(own(1), piece(b, 1), ss, rs.at[3], left)

    def ring_second(own, piece, ss, rs):
        right = {"tok": t_right}
        left = {"tok": t_left}
        rcopy(own(0), piece(b, 0), ss, rs.at[6], sib)
        rcopy(own(1), piece(b, 1), ss, rs.at[6], sib)
        rcopy(own(1), piece(b, 1), ss, rs.at[1], right)
        rcopy(own(0), piece(b, 0), ss, rs.at[2], left)

    def hand(piece, blk, h, ss, rs):
        rcopy(piece(blk, h), piece(blk, h), ss, rs.at[6], sib)

    def ring_mid(piece, ss, rs):
        bl = s * 4 + t_left
        br = s * 4 + t_right
        await_bytes(piece(bl, 0), rs.at[0])
        rcopy(piece(bl, 0), piece(bl, 0), ss, rs.at[4], {"tok": t_right})
        await_bytes(piece(br, 1), rs.at[3])
        rcopy(piece(br, 1), piece(br, 1), ss, rs.at[5], {"tok": t_left})
        hand(piece, bl, 0, ss, rs)
        hand(piece, br, 1, ss, rs)

    def ring_near(piece, ss, rs):
        bl = s * 4 + t_left
        br = s * 4 + t_right
        await_bytes(piece(bl, 1), rs.at[1])
        hand(piece, bl, 1, ss, rs)
        await_bytes(piece(br, 0), rs.at[2])
        hand(piece, br, 0, ss, rs)

    def ring_late(piece, ss, rs):
        bf = s * 4 + t_far
        await_bytes(piece(bf, 0), rs.at[4])
        hand(piece, bf, 0, ss, rs)
        await_bytes(piece(bf, 1), rs.at[5])
        hand(piece, bf, 1, ss, rs)

    def w_own(h):
        return w_ref.at[pl.ds(224 * h, 224), :]

    def w_piece(blk, h):
        return wf.at[pl.ds(pl.multiple_of(KB * blk + 224 * h, 32), 224), :]

    def l_piece(blk, h):
        return lg_all.at[pl.ds(512 * h, 512), pl.ds(pl.multiple_of(blk * T, T), T)]

    def l_own(h):
        return l_piece(b, h)

    pcopy = pltpu.make_async_copy(proj_ref, proj, loc_sem.at[0])
    pcopy.start()
    gather_y(ga, g1s, g1r)
    ring_start(w_own, w_piece, w_s, w_r)

    @pl.when(s == 0)
    def _():
        ring_second(w_own, w_piece, w_s, w_r)

    wcopy = pltpu.make_async_copy(w_ref, wf.at[pl.ds(pl.multiple_of(KB * b, 64), KB), :], loc_sem.at[1])
    wcopy.start()

    def normalize(g):
        def add(i, acc):
            for j in range(8):
                blk = g[i, j // 2, j % 2][:C, :].astype(F32)
                acc = acc + (blk * blk)
            return acc

        total = lax.fori_loop(0, 8, add, jnp.zeros((C, T), F32))
        inv = lax.rsqrt(jnp.sum(total, axis=0, keepdims=True) * (1.0 / D) + EPS)

        def scale(i, carry):
            parts = [g[i, j // 2, j % 2][:C, :].astype(F32) for j in range(8)]
            block = jnp.concatenate(parts, axis=0) * inv
            r = pl.multiple_of(i * KB, KB)
            normed[pl.ds(r, KB), :] = block
            rt[pl.ds(r, KB), :] = block.astype(BF)
            return carry

        lax.fori_loop(0, 8, scale, 0)
        return inv

    pcopy.wait()

    @pl.when(s == 1)
    def _():
        odd = lax.rem(z, 2) == 1

        def turn_proj(i, carry):
            r = pl.multiple_of(i * T, T)
            block = proj[:, pl.ds(r, T)].astype(F32)
            even_place = jnp.concatenate([block, jnp.zeros((T - C, T), F32)], axis=0)
            odd_place = jnp.concatenate([jnp.zeros((CP, T), F32), block, jnp.zeros((CP - C, T), F32)], axis=0)
            ph[pl.ds(r, T), :] = jnp.where(odd, odd_place, even_place).T.astype(BF)
            return carry

        lax.fori_loop(0, D // T, turn_proj, 0)
        for d in (4, 3, 5, 2, 6, 1, 7):
            zo = lax.rem(z + d, 8)
            rcopy(ph.at[pl.ds(pl.multiple_of(zo * KB, 64), KB), :], phr.at[z], p_s, p_r, at_z(d))
        phr[z] = ph[pl.ds(pl.multiple_of(z * KB, 64), KB), :]

    gather(ga, g1s, g1r, lambda: None)
    inv1 = normalize(ga)
    part = jnp.dot(proj[:, pl.ds(pl.multiple_of(s * D, D), D)], rt[...], preferred_element_type=F32)
    own_rows = pl.ds(pl.multiple_of(v * C, 8), C)

    @pl.when(s == 0)
    def _():
        xch[pl.ds(0, C), :] = part
        xch[pl.ds(C, 8), :] = jnp.broadcast_to(inv1, (8, T))
        xch[pl.ds(CP, C), :] = normed[own_rows, :]
        xch[pl.ds(CP + C, 8), :] = jnp.zeros((8, T), F32)
        rcopy(xch, xin, x_s.at[0], x_r.at[0], sib)
        inv_keep[...] = jnp.broadcast_to(inv1, (8, T))
        ring_mid(w_piece, w_s, w_r)
        ring_near(w_piece, w_s, w_r)

    @pl.when(s == 1)
    def _():
        await_bytes(xin, x_r.at[0])
        mixed = part + xin[pl.ds(0, C), :]
        gb[z, x, yl] = jnp.concatenate([mixed, jnp.zeros((CP - C, T), F32)], axis=0).astype(BF)
        rcopy(gb.at[z, x, yl], gb.at[z, x, yl], g2s.at[0], g2r.at[0], at_y)
        ring_second(w_own, w_piece, w_s, w_r)
        ring_mid(w_piece, w_s, w_r)
        await_bytes(gb.at[z, x, 1 - yl], g2r.at[0])
        gather(gb, g2s, g2r, lambda: None)
        ring_near(w_piece, w_s, w_r)
        inv_keep[...] = jnp.broadcast_to(normalize(gb), (8, T))
        await_bytes(phr.at[pl.ds(0, 7)], p_r)
        for i in range(4):
            pb[:, pl.ds(i * T, T)] = phr[2 * i] + phr[2 * i + 1]

    ring_late(w_piece, w_s, w_r)

    def turn(i, carry):
        r = pl.multiple_of(i * T, T)
        rnd[:, pl.ds(r, T)] = normed[pl.ds(r, T), :].T.astype(BF)
        return carry

    lax.fori_loop(0, D // T, turn, 0)
    wcopy.wait()
    await_bytes(wf.at[pl.ds(0, 4 * KB), :], w_r.at[6])

    part_rows = pl.ds(pl.multiple_of(x * SHARE, 16), SHARE)
    own_tokens = pl.ds(pl.multiple_of(b * T, T), T)

    def rows_of(o):
        return pl.ds(pl.multiple_of(o * KB + x * SHARE, 16), SHARE)

    def to_owner(d, carry):
        o = lax.rem(b + d, 8)
        rcopy(
            rt.at[rows_of(o), :], r_all.at[part_rows, own_tokens],
            r_s, r_r, {"section": lax.div(o, 4), "tok": lax.rem(o, 4)},
        )
        return carry

    def share_rows():
        await_bytes(r_all.at[part_rows, pl.ds(0, 7 * T)], r_r)
        for d in (2, 1, 3):
            rcopy(r_all.at[part_rows, :], r_all.at[part_rows, :], ra_s, ra_r, at_x(d))

    def logits_tile(i, carry):
        r = pl.multiple_of(i * 256, 256)
        tile = jnp.dot(rnd[...], wf[:, pl.ds(r, 256)], preferred_element_type=F32)
        logt[pl.ds(r, 256), :] = tile.T
        return carry

    lax.fori_loop(0, 4, logits_tile, 0)
    r_all[part_rows, own_tokens] = rt[rows_of(b), :]

    label = lab_ref[...] - v * VS
    place = lax.broadcasted_iota(jnp.int32, (VS, T), 0)
    hit = place == label
    values = logt[...]
    top = jnp.max(values, axis=0, keepdims=True)
    expo = jnp.exp(values - top)
    den = jnp.sum(expo, axis=0, keepdims=True)
    sel = jnp.sum(expo * values, axis=0, keepdims=True)
    lab = jnp.sum(jnp.where(hit, values, 0.0), axis=0, keepdims=True)

    def combine(slots):
        m = slots[0][0:1]
        for q in slots[1:]:
            m = jnp.maximum(m, q[0:1])
        d_ = jnp.zeros((1, T), F32)
        e_ = jnp.zeros((1, T), F32)
        l_ = jnp.zeros((1, T), F32)
        for q in slots:
            f = jnp.exp(q[0:1] - m)
            d_ = d_ + q[1:2] * f
            e_ = e_ + q[2:3] * f
            l_ = l_ + q[3:4]
        return jnp.concatenate([m, d_, e_, l_, jnp.zeros((4, T), F32)], axis=0)

    sx[xy] = jnp.concatenate([top, den, sel, lab, jnp.zeros((4, T), F32)], axis=0)
    for d in (4, 5, 3, 1, 7, 2, 6):
        rcopy(sx.at[xy], sx.at[xy], st_s.at[0], st_r.at[0], at_xy(d))
    lax.fori_loop(1, 8, to_owner, 0)
    await_bytes(sx.at[pl.ds(0, 7)], st_r.at[0])
    sz[z] = combine([sx[i] for i in range(8)])
    for d in (4, 3, 5, 2, 6, 1, 7):
        rcopy(sz.at[z], sz.at[z], st_s.at[1], st_r.at[1], at_z(d))
    await_bytes(sz.at[pl.ds(0, 7)], st_r.at[1])
    stats = combine([sz[i] for i in range(8)])
    weighting = jnp.where(s == 1, MTP_WEIGHT, 1.0).astype(F32)
    inv_den = 1.0 / stats[1:2]
    mean_dot = weighting * (stats[2:3] * inv_den - stats[3:4]) * (1.0 / D)
    prob = jnp.exp(logt[...] - stats[0:1]) * inv_den
    lgt = (weighting * (prob - hit.astype(F32))).astype(BF)
    lg_all[:, pl.ds(pl.multiple_of(b * T, T), T)] = lgt

    ring_start(l_own, l_piece, l_s, l_r)
    pad = jnp.zeros((CP - C, T), F32)

    def spread(block, p, i):
        for j in range(8):
            p[i, j // 2, j % 2] = jnp.concatenate([block[C * j:C * (j + 1), :], pad], axis=0).astype(BF)

    def group(d):
        return lax.rem(lax.div(z, GROUP) + d, GROUPS)

    def blocks(d):
        return pl.ds(pl.multiple_of(group(d) * GROUP, GROUP), GROUP)

    def scatter_x(make, p, rx, ss, rs):
        for n in range(GROUPS):
            d = GROUPS - 1 - n
            for k in range(GROUP):
                make(group(d) * GROUP + k)
            for dx in (2, 1, 3):
                xo = lax.rem(x + dx, 4)
                rcopy(p.at[blocks(d), xo], rx.at[x, blocks(d)], ss, rs.at[d], at_x(dx))

    def scatter_zy(p, rx, az, af, rz, ss, rs, ss2, rs2):
        for n in range(GROUPS):
            d = GROUPS - 1 - n
            await_bytes(rx.at[pl.ds(0, 3), blocks(d)], rs.at[d])
            for k in range(GROUP):
                i = group(d) * GROUP + k
                for j in range(2):
                    a = p[i, x, j].astype(F32)
                    for dx in range(1, 4):
                        a = a + rx[lax.rem(x + dx, 4), i, j].astype(F32)
                    e = i * 2 + j
                    af[e] = a
                    az[e] = a.astype(BF)

                    @pl.when(e != zy)
                    def _():
                        rcopy(az.at[e], rz.at[zy], ss2, rs2, vocab_of(e))
        ring_second(l_own, l_piece, l_s, l_r)
        ring_mid(l_piece, l_s, l_r)
        share_rows()
        await_bytes(rz.at[pl.ds(0, 15)], rs2)
        a = af[zy]
        for d in range(1, 16):
            a = a + rz[lax.rem(zy + d, 16)].astype(F32)
        return a[:C, :]

    def scatter_sent(rx, rz, ss, ss2):
        await_bytes(rx.at[pl.ds(0, 3)], ss)
        await_bytes(rz.at[pl.ds(0, 15)], ss2)

    def feature(i):
        block = jnp.dot(wf[pl.ds(pl.multiple_of(i * KB, KB), KB), :], lgt, preferred_element_type=F32)
        spread(block, p3, i)

    scatter_x(feature, p3, rx3, q3s.at[0], q3r)
    fgrad = scatter_zy(p3, rx3, az3, af3, rz3, q3s.at[0], q3r, q3s.at[1], q3r.at[8])
    back = (fgrad - normed[own_rows, :] * mean_dot) * inv_keep[0:1]

    def head_grad():
        await_bytes(r_all.at[pl.ds(0, 3 * SHARE), :], ra_r)
        ring_near(l_piece, l_s, l_r)
        ring_late(l_piece, l_s, l_r)
        await_bytes(lg_all.at[:, pl.ds(0, 4 * T)], l_r.at[6])

        def tile(i, carry):
            r = pl.multiple_of(i * 256, 256)
            g = lax.dot_general(
                r_all[...], lg_all[pl.ds(r, 256), :], (((1,), (1,)), ((), ())), preferred_element_type=F32
            )
            hg_ref[:, pl.ds(r, 256)] = g.astype(BF)
            return carry

        lax.fori_loop(0, 4, tile, 0)

    @pl.when(s == 0)
    def _():
        bk[...] = back
        rcopy(bk, bkin, x_s.at[1], x_r.at[1], sib)
        head_grad()
        await_bytes(bkin, x_r.at[1])
        out_ref[...] = back + bkin[...]
        await_bytes(xch, x_s.at[0])

    @pl.when(s == 1)
    def _():
        mg = back.astype(BF)
        hdot = jnp.sum(mg.astype(F32) * xin[pl.ds(0, C), :], axis=0, keepdims=True)
        high = hdot.astype(BF).astype(F32)
        middle = (hdot - high).astype(BF).astype(F32)
        low = hdot - high - middle
        mgb[z] = jnp.concatenate(
            [mg.astype(F32), high, middle, low, jnp.zeros((5, T), F32)], axis=0
        ).astype(BF)
        for d in (4, 3, 5, 2, 6, 1, 7):
            rcopy(mgb.at[z], mgb.at[z], m_s, m_r, at_z(d))
        await_bytes(mgb.at[pl.ds(0, 7)], m_r)
        hsum = jnp.zeros((8, T), F32)
        for i in range(8):
            hsum = hsum + mgb[i, pl.ds(C - 8, 16), :].astype(F32)[8:16]
        hrow = hsum[0:1] + hsum[1:2] + hsum[2:3]
        joint = jnp.dot(pb[...], mgb[...].reshape(8 * CP, T), preferred_element_type=F32)
        for j in range(8):
            jb[j] = jnp.concatenate([joint[C * j:C * (j + 1), :], jnp.broadcast_to(hrow, (8, T))], axis=0)
        for d in (4, 5, 3, 1, 7, 2, 6):
            rcopy(jb.at[lax.rem(xy + d, 8)], jx.at[xy], j_s, j_r, at_xy(d))
        await_bytes(jx.at[pl.ds(0, 7)], j_r)
        tot = jb[xy]
        for d in range(1, 8):
            tot = tot + jx[lax.rem(xy + d, 8)]
        jgrad = tot[:C, :]
        hmean = tot[C:C + 1] * (1.0 / D)
        depth = (jgrad - xin[pl.ds(CP, C), :] * hmean) * xin[pl.ds(C, 1), :]
        bk[...] = depth
        rcopy(bk, bkin, x_s.at[1], x_r.at[1], sib)
        await_bytes(bkin, x_r.at[1])
        out_ref[...] = bkin[...] + depth
        head_grad()
        gather_sent(gb, g2s)
        await_bytes(mgb.at[pl.ds(0, 7)], m_s)
        await_bytes(jx.at[pl.ds(0, 7)], j_s)
        await_bytes(phr.at[pl.ds(0, 7)], p_s)

    await_bytes(bk, x_s.at[1])
    gather_sent(ga, g1s)
    scatter_sent(rx3, rz3, q3s.at[0], q3s.at[1])
    await_bytes(sx.at[pl.ds(0, 7)], st_s.at[0])
    await_bytes(sz.at[pl.ds(0, 7)], st_s.at[1])
    await_bytes(r_all.at[part_rows, pl.ds(0, 7 * T)], r_s)
    await_bytes(r_all.at[pl.ds(0, 3 * SHARE), :], ra_s)
    await_bytes(wf.at[pl.ds(0, 7 * KB), :], w_s)
    await_bytes(lg_all.at[:, pl.ds(0, 7 * T)], l_s)


def local(rows, targets, proj_weight, head_weight):
    vm = pl.BlockSpec(memory_space=pltpu.VMEM)
    anyspace = pl.BlockSpec(memory_space=pl.ANY)
    dma = pltpu.SemaphoreType.DMA

    def rs_bufs():
        return [
            pltpu.VMEM((8, 4, 2, CP, T), BF),
            pltpu.VMEM((4, 8, 2, CP, T), BF),
            pltpu.VMEM((16, CP, T), BF),
            pltpu.VMEM((16, CP, T), F32),
            pltpu.VMEM((16, CP, T), BF),
        ]

    head_grad, grad_t = pl.pallas_call(
        kernel,
        out_shape=(
            jax.ShapeDtypeStruct((KB, VS), BF),
            jax.ShapeDtypeStruct((C, T), F32),
        ),
        in_specs=[vm, vm, anyspace, anyspace],
        out_specs=(vm, vm),
        scratch_shapes=[
            pltpu.VMEM((D, VS), BF),
            pltpu.VMEM((C, 2 * D), BF),
            pltpu.VMEM((D, T), BF),
            pltpu.VMEM((8, 4, 2, CP, T), BF),
            pltpu.VMEM((8, 4, 2, CP, T), BF),
            pltpu.VMEM((D, T), F32),
            pltpu.VMEM((D, T), BF),
            pltpu.VMEM((T, D), BF),
            pltpu.VMEM((VS, T), F32),
            pltpu.VMEM((VS, 8 * T), BF),
            pltpu.VMEM((KB, 8 * T), BF),
            *rs_bufs(),
            pltpu.VMEM((8, KB, T), BF),
            pltpu.VMEM((KB, 8 * CP), BF),
            pltpu.VMEM((8, CP, T), BF),
            pltpu.VMEM((8, CP, T), F32),
            pltpu.VMEM((8, CP, T), F32),
            pltpu.VMEM((8, 8, T), F32),
            pltpu.VMEM((8, 8, T), F32),
            pltpu.VMEM((8, T), F32),
            pltpu.VMEM((2 * CP, T), F32),
            pltpu.VMEM((2 * CP, T), F32),
            pltpu.VMEM((C, T), F32),
            pltpu.VMEM((C, T), F32),
            dma((2,)), dma, dma((7,)), dma, dma((7,)), dma, dma,
            dma((3,)), dma((6,)), dma((3,)), dma((6,)),
            dma((2,)), dma((2,)), dma((2,)), dma((9,)),
            dma, dma, dma, dma, dma, dma, dma, dma,
            dma((2,)), dma((2,)),
        ],
        compiler_params=pltpu.CompilerParams(
            collective_id=0, has_side_effects=True, vmem_limit_bytes=56 * 1024 * 1024
        ),
        cost_estimate=pl.CostEstimate(flops=3 * 10**9, bytes_accessed=2 * 10**7, transcendentals=3 * 10**5),
        name="head",
    )(jnp.swapaxes(rows, 1, 2), targets, proj_weight.T, head_weight)
    return head_grad, grad_t.T


def solution(mesh):
    placed = (
        P("section", "tok", "vocab"),
        P("section", "tok"),
        P(None, "vocab"),
        P(("section", "tok"), "vocab"),
    )
    return jax.shard_map(
        local,
        mesh=mesh,
        in_specs=placed,
        out_specs=(P(("section", "tok"), "vocab"), P("tok", "vocab")),
        check_vma=False,
    )
```

```python
import jax
import jax.numpy as jnp
from jax import lax
from jax.experimental import pallas as pl
from jax.experimental.pallas import tpu as pltpu
from jax.sharding import PartitionSpec as P

EPS = 1e-06
MTP_WEIGHT = 0.3
D = 3584
T = 128
C = 56
CP = 64
VS = 1024
KB = 448
SHARE = KB // 4
MESH = pl.DeviceIdType.MESH
ORDER = (8, 7, 9, 6, 10, 5, 11, 4, 12, 3, 13, 2, 14, 1, 15)
GROUP = 1
GROUPS = 8 // GROUP
BF = jnp.bfloat16
F32 = jnp.float32


def rcopy(src, dst, ssem, rsem, dev):
    copy = pltpu.make_async_remote_copy(
        src_ref=src, dst_ref=dst, send_sem=ssem, recv_sem=rsem, device_id=dev, device_id_type=MESH
    )
    copy.start()


def await_bytes(ref, sem):
    pltpu.make_async_copy(ref, ref, sem).wait()


def kernel(
    rows_ref, lab_ref, proj_ref, w_ref, hg_ref, out_ref,
    wf, proj, ph, ga, gb, normed, rt, rnd, logt, lg_all, r_all,
    p3, rx3, az3, af3, rz3,
    phr, pb, mgb, jb, jx, sx, sz, inv_keep,
    xch, xin, bk, bkin,
    loc_sem, w_s, w_r, l_s, l_r, r_s, r_r,
    g1s, g1r, g2s, g2r, st_s, st_r, q3s, q3r, p_s, p_r, m_s, m_r, j_s, j_r, ra_s, ra_r, x_s, x_r,
):
    s = lax.axis_index("section")
    v = lax.axis_index("vocab")
    t = lax.axis_index("tok")
    z = lax.div(v, 8)
    x = lax.rem(lax.div(v, 2), 4)
    yl = lax.rem(v, 2)
    b = s * 4 + t
    sib = {"section": 1 - s}
    t_right = lax.rem(t + 1, 4)
    t_left = lax.rem(t + 3, 4)
    t_far = lax.rem(t + 2, 4)

    def at_z(d):
        return {"vocab": lax.rem(z + d, 8) * 8 + x * 2 + yl}

    def at_x(d):
        return {"vocab": z * 8 + lax.rem(x + d, 4) * 2 + yl}

    zy = z * 2 + yl

    def vocab_of(e):
        return {"vocab": lax.div(e, 2) * 8 + x * 2 + lax.rem(e, 2)}

    def at_zy(d):
        return vocab_of(lax.rem(zy + d, 16))

    xy = x * 2 + yl

    def at_xy(d):
        return {"vocab": z * 8 + lax.rem(xy + d, 8)}

    at_y = {"vocab": z * 8 + x * 2 + (1 - yl)}

    barrier = pltpu.get_barrier_semaphore()
    for d in range(1, 16):
        pl.semaphore_signal(barrier, inc=1, device_id=at_zy(d), device_id_type=MESH)
    for d in range(1, 8):
        pl.semaphore_signal(barrier, inc=1, device_id=at_xy(d), device_id_type=MESH)
    for d in range(1, 8):
        o = lax.rem(b + d, 8)
        pl.semaphore_signal(
            barrier, inc=1, device_id={"section": lax.div(o, 4), "tok": lax.rem(o, 4)}, device_id_type=MESH
        )
    own_t = rows_ref[0].astype(F32)
    ga[z, x, yl] = jnp.concatenate([own_t, jnp.zeros((CP - C, T), F32)], axis=0).astype(BF)
    pl.semaphore_wait(barrier, 29)

    def gather_y(g, ss, rs):
        rcopy(g.at[z, x, yl], g.at[z, x, yl], ss.at[0], rs.at[0], at_y)
        await_bytes(g.at[z, x, 1 - yl], rs.at[0])

    def gather(g, ss, rs, between):
        for d in (4, 3, 5, 2, 6, 1, 7):
            rcopy(g.at[z, x], g.at[z, x], ss.at[1], rs.at[1], at_z(d))
        between()
        await_bytes(g.at[pl.ds(0, 7), x], rs.at[1])
        xl = lax.rem(x + 3, 4)
        xr = lax.rem(x + 1, 4)
        rcopy(g.at[:, x], g.at[:, x], ss.at[2], rs.at[2], at_x(1))
        rcopy(g.at[:, x], g.at[:, x], ss.at[2], rs.at[3], at_x(3))
        await_bytes(g.at[:, xl], rs.at[2])
        lo = pl.ds(0, 4)
        hi = pl.ds(4, 4)
        rcopy(g.at[lo, xl], g.at[lo, xl], ss.at[2], rs.at[4], at_x(1))
        await_bytes(g.at[:, xr], rs.at[3])
        rcopy(g.at[hi, xr], g.at[hi, xr], ss.at[2], rs.at[5], at_x(3))
        await_bytes(g.at[lo, x], rs.at[4])
        await_bytes(g.at[hi, x], rs.at[5])

    def gather_sent(g, ss):
        await_bytes(g.at[z, x, yl], ss.at[0])
        await_bytes(g.at[pl.ds(0, 7), x], ss.at[1])
        await_bytes(g.at[:, pl.ds(0, 3)], ss.at[2])

    def ring_start(own, piece, ss, rs):
        right = {"tok": t_right}
        left = {"tok": t_left}
        rcopy(own(0), piece(b, 0), ss, rs.at[0], right)
        rcopy(own(1), piece(b, 1), ss, rs.at[3], left)

    def ring_second(own, piece, ss, rs):
        right = {"tok": t_right}
        left = {"tok": t_left}
        rcopy(own(0), piece(b, 0), ss, rs.at[6], sib)
        rcopy(own(1), piece(b, 1), ss, rs.at[6], sib)
        rcopy(own(1), piece(b, 1), ss, rs.at[1], right)
        rcopy(own(0), piece(b, 0), ss, rs.at[2], left)

    def hand(piece, blk, h, ss, rs):
        rcopy(piece(blk, h), piece(blk, h), ss, rs.at[6], sib)

    def ring_mid(piece, ss, rs):
        bl = s * 4 + t_left
        br = s * 4 + t_right
        await_bytes(piece(bl, 0), rs.at[0])
        for q in range(2):
            rcopy(piece(bl, 0, q), piece(bl, 0, q), ss, rs.at[4 + 3 * q], {"tok": t_right})
        await_bytes(piece(br, 1), rs.at[3])
        for q in range(2):
            rcopy(piece(br, 1, q), piece(br, 1, q), ss, rs.at[5 + 3 * q], {"tok": t_left})
        hand(piece, bl, 0, ss, rs)
        hand(piece, br, 1, ss, rs)

    def ring_near(piece, ss, rs):
        bl = s * 4 + t_left
        br = s * 4 + t_right
        await_bytes(piece(bl, 1), rs.at[1])
        hand(piece, bl, 1, ss, rs)
        await_bytes(piece(br, 0), rs.at[2])
        hand(piece, br, 0, ss, rs)

    def ring_late(piece, ss, rs):
        bf = s * 4 + t_far
        for q in range(2):
            for h in range(2):
                await_bytes(piece(bf, h, q), rs.at[4 + h + 3 * q])
                rcopy(piece(bf, h, q), piece(bf, h, q), ss, rs.at[6], sib)

    def w_own(h):
        return w_ref.at[pl.ds(224 * h, 224), :]

    def w_piece(blk, h, q=None):
        first, count = (224 * h, 224) if q is None else (224 * h + 112 * q, 112)
        return wf.at[pl.ds(pl.multiple_of(KB * blk + first, 16), count), :]

    def l_piece(blk, h, q=None):
        first, count = (512 * h, 512) if q is None else (512 * h + 256 * q, 256)
        return lg_all.at[pl.ds(first, count), pl.ds(pl.multiple_of(blk * T, T), T)]

    def l_own(h):
        return l_piece(b, h)

    pcopy = pltpu.make_async_copy(proj_ref, proj, loc_sem.at[0])
    pcopy.start()
    gather_y(ga, g1s, g1r)
    ring_start(w_own, w_piece, w_s, w_r)

    @pl.when(s == 0)
    def _():
        ring_second(w_own, w_piece, w_s, w_r)

    wcopy = pltpu.make_async_copy(w_ref, wf.at[pl.ds(pl.multiple_of(KB * b, 64), KB), :], loc_sem.at[1])
    wcopy.start()

    def normalize(g):
        def add(i, acc):
            for j in range(8):
                blk = g[i, j // 2, j % 2][:C, :].astype(F32)
                acc = acc + (blk * blk)
            return acc

        total = lax.fori_loop(0, 8, add, jnp.zeros((C, T), F32))
        inv = lax.rsqrt(jnp.sum(total, axis=0, keepdims=True) * (1.0 / D) + EPS)

        def scale(i, carry):
            parts = [g[i, j // 2, j % 2][:C, :].astype(F32) for j in range(8)]
            block = jnp.concatenate(parts, axis=0) * inv
            r = pl.multiple_of(i * KB, KB)
            normed[pl.ds(r, KB), :] = block
            rt[pl.ds(r, KB), :] = block.astype(BF)
            return carry

        lax.fori_loop(0, 8, scale, 0)
        return inv

    def share_proj():
        pcopy.wait()

        @pl.when(s == 1)
        def _():
            odd = lax.rem(z, 2) == 1

            def turn_proj(i, carry):
                r = pl.multiple_of(i * T, T)
                block = proj[:, pl.ds(r, T)].astype(F32)
                even_place = jnp.concatenate([block, jnp.zeros((T - C, T), F32)], axis=0)
                odd_place = jnp.concatenate([jnp.zeros((CP, T), F32), block, jnp.zeros((CP - C, T), F32)], axis=0)
                ph[pl.ds(r, T), :] = jnp.where(odd, odd_place, even_place).T.astype(BF)
                return carry

            lax.fori_loop(0, D // T, turn_proj, 0)
            for d in (4, 3, 5, 2, 6, 1, 7):
                zo = lax.rem(z + d, 8)
                rcopy(ph.at[pl.ds(pl.multiple_of(zo * KB, 64), KB), :], phr.at[z], p_s, p_r, at_z(d))
            phr[z] = ph[pl.ds(pl.multiple_of(z * KB, 64), KB), :]

    gather(ga, g1s, g1r, share_proj)
    inv1 = normalize(ga)
    part = jnp.dot(proj[:, pl.ds(pl.multiple_of(s * D, D), D)], rt[...], preferred_element_type=F32)
    own_rows = pl.ds(pl.multiple_of(v * C, 8), C)

    @pl.when(s == 0)
    def _():
        xch[pl.ds(0, C), :] = part
        xch[pl.ds(C, 8), :] = jnp.broadcast_to(inv1, (8, T))
        xch[pl.ds(CP, C), :] = normed[own_rows, :]
        xch[pl.ds(CP + C, 8), :] = jnp.zeros((8, T), F32)
        rcopy(xch, xin, x_s.at[0], x_r.at[0], sib)
        inv_keep[...] = jnp.broadcast_to(inv1, (8, T))
        ring_mid(w_piece, w_s, w_r)
        ring_near(w_piece, w_s, w_r)

    @pl.when(s == 1)
    def _():
        await_bytes(xin, x_r.at[0])
        mixed = part + xin[pl.ds(0, C), :]
        gb[z, x, yl] = jnp.concatenate([mixed, jnp.zeros((CP - C, T), F32)], axis=0).astype(BF)
        rcopy(gb.at[z, x, yl], gb.at[z, x, yl], g2s.at[0], g2r.at[0], at_y)
        ring_second(w_own, w_piece, w_s, w_r)
        ring_mid(w_piece, w_s, w_r)
        await_bytes(gb.at[z, x, 1 - yl], g2r.at[0])
        gather(gb, g2s, g2r, lambda: None)
        ring_near(w_piece, w_s, w_r)
        inv_keep[...] = jnp.broadcast_to(normalize(gb), (8, T))
        await_bytes(phr.at[pl.ds(0, 7)], p_r)
        for i in range(4):
            pb[:, pl.ds(i * T, T)] = phr[2 * i] + phr[2 * i + 1]

    ring_late(w_piece, w_s, w_r)

    def turn(i, carry):
        r = pl.multiple_of(i * T, T)
        rnd[:, pl.ds(r, T)] = normed[pl.ds(r, T), :].T.astype(BF)
        return carry

    lax.fori_loop(0, D // T, turn, 0)
    wcopy.wait()
    await_bytes(wf.at[pl.ds(0, 4 * KB), :], w_r.at[6])

    part_rows = pl.ds(pl.multiple_of(x * SHARE, 16), SHARE)
    own_tokens = pl.ds(pl.multiple_of(b * T, T), T)

    def rows_of(o):
        return pl.ds(pl.multiple_of(o * KB + x * SHARE, 16), SHARE)

    def to_owner(d, carry):
        o = lax.rem(b + d, 8)
        rcopy(
            rt.at[rows_of(o), :], r_all.at[part_rows, own_tokens],
            r_s, r_r, {"section": lax.div(o, 4), "tok": lax.rem(o, 4)},
        )
        return carry

    def share_rows():
        await_bytes(r_all.at[part_rows, pl.ds(0, 7 * T)], r_r)
        for d in (2, 1, 3):
            rcopy(r_all.at[part_rows, :], r_all.at[part_rows, :], ra_s, ra_r, at_x(d))

    def logits_tile(i, carry):
        r = pl.multiple_of(i * 256, 256)
        tile = jnp.dot(rnd[...], wf[:, pl.ds(r, 256)], preferred_element_type=F32)
        logt[pl.ds(r, 256), :] = tile.T
        return carry

    lax.fori_loop(0, 4, logits_tile, 0)
    r_all[part_rows, own_tokens] = rt[rows_of(b), :]

    label = lab_ref[...] - v * VS
    place = lax.broadcasted_iota(jnp.int32, (VS, T), 0)
    hit = place == label
    values = logt[...]
    top = jnp.max(values, axis=0, keepdims=True)
    expo = jnp.exp(values - top)
    den = jnp.sum(expo, axis=0, keepdims=True)
    sel = jnp.sum(expo * values, axis=0, keepdims=True)
    lab = jnp.sum(jnp.where(hit, values, 0.0), axis=0, keepdims=True)

    def combine(slots):
        m = slots[0][0:1]
        for q in slots[1:]:
            m = jnp.maximum(m, q[0:1])
        d_ = jnp.zeros((1, T), F32)
        e_ = jnp.zeros((1, T), F32)
        l_ = jnp.zeros((1, T), F32)
        for q in slots:
            f = jnp.exp(q[0:1] - m)
            d_ = d_ + q[1:2] * f
            e_ = e_ + q[2:3] * f
            l_ = l_ + q[3:4]
        return jnp.concatenate([m, d_, e_, l_, jnp.zeros((4, T), F32)], axis=0)

    sx[xy] = jnp.concatenate([top, den, sel, lab, jnp.zeros((4, T), F32)], axis=0)
    for d in (4, 5, 3, 1, 7, 2, 6):
        rcopy(sx.at[xy], sx.at[xy], st_s.at[0], st_r.at[0], at_xy(d))
    lax.fori_loop(1, 8, to_owner, 0)
    await_bytes(sx.at[pl.ds(0, 7)], st_r.at[0])
    sz[z] = combine([sx[i] for i in range(8)])
    for d in (4, 3, 5, 2, 6, 1, 7):
        rcopy(sz.at[z], sz.at[z], st_s.at[1], st_r.at[1], at_z(d))
    await_bytes(sz.at[pl.ds(0, 7)], st_r.at[1])
    stats = combine([sz[i] for i in range(8)])
    weighting = jnp.where(s == 1, MTP_WEIGHT, 1.0).astype(F32)
    inv_den = 1.0 / stats[1:2]
    mean_dot = weighting * (stats[2:3] * inv_den - stats[3:4]) * (1.0 / D)
    prob = jnp.exp(logt[...] - stats[0:1]) * inv_den
    lgt = (weighting * (prob - hit.astype(F32))).astype(BF)
    lg_all[:, pl.ds(pl.multiple_of(b * T, T), T)] = lgt

    ring_start(l_own, l_piece, l_s, l_r)

    @pl.when(s == 0)
    def _():
        ring_second(l_own, l_piece, l_s, l_r)

    pad = jnp.zeros((CP - C, T), F32)

    def spread(block, p, i):
        for j in range(8):
            p[i, j // 2, j % 2] = jnp.concatenate([block[C * j:C * (j + 1), :], pad], axis=0).astype(BF)

    def group(d):
        return lax.rem(lax.div(z, GROUP) + d, GROUPS)

    def blocks(d):
        return pl.ds(pl.multiple_of(group(d) * GROUP, GROUP), GROUP)

    def scatter_x(make, p, rx, ss, rs):
        for n in range(GROUPS):
            d = GROUPS - 1 - n
            for k in range(GROUP):
                make(group(d) * GROUP + k)
            for dx in (2, 1, 3):
                xo = lax.rem(x + dx, 4)
                rcopy(p.at[blocks(d), xo], rx.at[x, blocks(d)], ss, rs.at[d], at_x(dx))

    def scatter_zy(p, rx, az, af, rz, ss, rs, ss2, rs2):
        for n in range(GROUPS):
            d = GROUPS - 1 - n
            await_bytes(rx.at[pl.ds(0, 3), blocks(d)], rs.at[d])
            for k in range(GROUP):
                i = group(d) * GROUP + k
                for j in range(2):
                    a = p[i, x, j].astype(F32)
                    for dx in range(1, 4):
                        a = a + rx[lax.rem(x + dx, 4), i, j].astype(F32)
                    e = i * 2 + j
                    af[e] = a
                    az[e] = a.astype(BF)

                    @pl.when(e != zy)
                    def _():
                        rcopy(az.at[e], rz.at[zy], ss2, rs2, vocab_of(e))
        @pl.when(s == 1)
        def _():
            ring_second(l_own, l_piece, l_s, l_r)

        ring_mid(l_piece, l_s, l_r)
        share_rows()
        await_bytes(rz.at[pl.ds(0, 15)], rs2)
        a = af[zy]
        for d in range(1, 16):
            a = a + rz[lax.rem(zy + d, 16)].astype(F32)
        return a[:C, :]

    def scatter_sent(rx, rz, ss, ss2):
        await_bytes(rx.at[pl.ds(0, 3)], ss)
        await_bytes(rz.at[pl.ds(0, 15)], ss2)

    def feature(i):
        block = jnp.dot(wf[pl.ds(pl.multiple_of(i * KB, KB), KB), :], lgt, preferred_element_type=F32)
        spread(block, p3, i)

    scatter_x(feature, p3, rx3, q3s.at[0], q3r)
    fgrad = scatter_zy(p3, rx3, az3, af3, rz3, q3s.at[0], q3r, q3s.at[1], q3r.at[8])
    back = (fgrad - normed[own_rows, :] * mean_dot) * inv_keep[0:1]

    def head_grad():
        await_bytes(r_all.at[pl.ds(0, 3 * SHARE), :], ra_r)
        ring_near(l_piece, l_s, l_r)
        ring_late(l_piece, l_s, l_r)
        await_bytes(lg_all.at[:, pl.ds(0, 4 * T)], l_r.at[6])

        def tile(i, carry):
            r = pl.multiple_of(i * 256, 256)
            g = lax.dot_general(
                r_all[...], lg_all[pl.ds(r, 256), :], (((1,), (1,)), ((), ())), preferred_element_type=F32
            )
            hg_ref[:, pl.ds(r, 256)] = g.astype(BF)
            return carry

        lax.fori_loop(0, 4, tile, 0)

    @pl.when(s == 0)
    def _():
        bk[...] = back
        rcopy(bk, bkin, x_s.at[1], x_r.at[1], sib)
        head_grad()
        await_bytes(bkin, x_r.at[1])
        out_ref[...] = back + bkin[...]
        await_bytes(xch, x_s.at[0])

    @pl.when(s == 1)
    def _():
        mg = back.astype(BF)
        hdot = jnp.sum(mg.astype(F32) * xin[pl.ds(0, C), :], axis=0, keepdims=True)
        high = hdot.astype(BF).astype(F32)
        middle = (hdot - high).astype(BF).astype(F32)
        low = hdot - high - middle
        mgb[z] = jnp.concatenate(
            [mg.astype(F32), high, middle, low, jnp.zeros((5, T), F32)], axis=0
        ).astype(BF)
        for d in (4, 3, 5, 2, 6, 1, 7):
            rcopy(mgb.at[z], mgb.at[z], m_s, m_r, at_z(d))
        await_bytes(mgb.at[pl.ds(0, 7)], m_r)
        hsum = jnp.zeros((8, T), F32)
        for i in range(8):
            hsum = hsum + mgb[i, pl.ds(C - 8, 16), :].astype(F32)[8:16]
        hrow = hsum[0:1] + hsum[1:2] + hsum[2:3]
        joint = jnp.dot(pb[...], mgb[...].reshape(8 * CP, T), preferred_element_type=F32)
        for j in range(8):
            jb[j] = jnp.concatenate([joint[C * j:C * (j + 1), :], jnp.broadcast_to(hrow, (8, T))], axis=0)
        for d in (4, 5, 3, 1, 7, 2, 6):
            rcopy(jb.at[lax.rem(xy + d, 8)], jx.at[xy], j_s, j_r, at_xy(d))
        await_bytes(jx.at[pl.ds(0, 7)], j_r)
        tot = jb[xy]
        for d in range(1, 8):
            tot = tot + jx[lax.rem(xy + d, 8)]
        jgrad = tot[:C, :]
        hmean = tot[C:C + 1] * (1.0 / D)
        depth = (jgrad - xin[pl.ds(CP, C), :] * hmean) * xin[pl.ds(C, 1), :]
        bk[...] = depth
        rcopy(bk, bkin, x_s.at[1], x_r.at[1], sib)
        await_bytes(bkin, x_r.at[1])
        out_ref[...] = bkin[...] + depth
        head_grad()
        gather_sent(gb, g2s)
        await_bytes(mgb.at[pl.ds(0, 7)], m_s)
        await_bytes(jx.at[pl.ds(0, 7)], j_s)
        await_bytes(phr.at[pl.ds(0, 7)], p_s)

    await_bytes(bk, x_s.at[1])
    gather_sent(ga, g1s)
    scatter_sent(rx3, rz3, q3s.at[0], q3s.at[1])
    await_bytes(sx.at[pl.ds(0, 7)], st_s.at[0])
    await_bytes(sz.at[pl.ds(0, 7)], st_s.at[1])
    await_bytes(r_all.at[part_rows, pl.ds(0, 7 * T)], r_s)
    await_bytes(r_all.at[pl.ds(0, 3 * SHARE), :], ra_s)
    await_bytes(wf.at[pl.ds(0, 7 * KB), :], w_s)
    await_bytes(lg_all.at[:, pl.ds(0, 7 * T)], l_s)


def local(rows, targets, proj_weight, head_weight):
    vm = pl.BlockSpec(memory_space=pltpu.VMEM)
    anyspace = pl.BlockSpec(memory_space=pl.ANY)
    dma = pltpu.SemaphoreType.DMA

    def rs_bufs():
        return [
            pltpu.VMEM((8, 4, 2, CP, T), BF),
            pltpu.VMEM((4, 8, 2, CP, T), BF),
            pltpu.VMEM((16, CP, T), BF),
            pltpu.VMEM((16, CP, T), F32),
            pltpu.VMEM((16, CP, T), BF),
        ]

    head_grad, grad_t = pl.pallas_call(
        kernel,
        out_shape=(
            jax.ShapeDtypeStruct((KB, VS), BF),
            jax.ShapeDtypeStruct((C, T), F32),
        ),
        in_specs=[vm, vm, anyspace, anyspace],
        out_specs=(vm, vm),
        scratch_shapes=[
            pltpu.VMEM((D, VS), BF),
            pltpu.VMEM((C, 2 * D), BF),
            pltpu.VMEM((D, T), BF),
            pltpu.VMEM((8, 4, 2, CP, T), BF),
            pltpu.VMEM((8, 4, 2, CP, T), BF),
            pltpu.VMEM((D, T), F32),
            pltpu.VMEM((D, T), BF),
            pltpu.VMEM((T, D), BF),
            pltpu.VMEM((VS, T), F32),
            pltpu.VMEM((VS, 8 * T), BF),
            pltpu.VMEM((KB, 8 * T), BF),
            *rs_bufs(),
            pltpu.VMEM((8, KB, T), BF),
            pltpu.VMEM((KB, 8 * CP), BF),
            pltpu.VMEM((8, CP, T), BF),
            pltpu.VMEM((8, CP, T), F32),
            pltpu.VMEM((8, CP, T), F32),
            pltpu.VMEM((8, 8, T), F32),
            pltpu.VMEM((8, 8, T), F32),
            pltpu.VMEM((8, T), F32),
            pltpu.VMEM((2 * CP, T), F32),
            pltpu.VMEM((2 * CP, T), F32),
            pltpu.VMEM((C, T), F32),
            pltpu.VMEM((C, T), F32),
            dma((2,)), dma, dma((9,)), dma, dma((9,)), dma, dma,
            dma((3,)), dma((6,)), dma((3,)), dma((6,)),
            dma((2,)), dma((2,)), dma((2,)), dma((9,)),
            dma, dma, dma, dma, dma, dma, dma, dma,
            dma((2,)), dma((2,)),
        ],
        compiler_params=pltpu.CompilerParams(
            collective_id=0, has_side_effects=True, vmem_limit_bytes=56 * 1024 * 1024
        ),
        cost_estimate=pl.CostEstimate(flops=3 * 10**9, bytes_accessed=2 * 10**7, transcendentals=3 * 10**5),
        name="head",
    )(jnp.swapaxes(rows, 1, 2), targets, proj_weight.T, head_weight)
    return head_grad, grad_t.T


def solution(mesh):
    placed = (
        P("section", "tok", "vocab"),
        P("section", "tok"),
        P(None, "vocab"),
        P(("section", "tok"), "vocab"),
    )
    return jax.shard_map(
        local,
        mesh=mesh,
        in_specs=placed,
        out_specs=(P(("section", "tok"), "vocab"), P("tok", "vocab")),
        check_vma=False,
    )
```

```python
import jax
import jax.numpy as jnp
from jax import lax
from jax.experimental import pallas as pl
from jax.experimental.pallas import tpu as pltpu
from jax.sharding import PartitionSpec as P

EPS = 1e-06
MTP_WEIGHT = 0.3
D = 3584
T = 128
C = 56
CP = 64
VS = 1024
KB = 448
SHARE = KB // 4
MESH = pl.DeviceIdType.MESH
ORDER = (8, 7, 9, 6, 10, 5, 11, 4, 12, 3, 13, 2, 14, 1, 15)
GROUP = 1
GROUPS = 8 // GROUP
BF = jnp.bfloat16
F32 = jnp.float32


def rcopy(src, dst, ssem, rsem, dev):
    copy = pltpu.make_async_remote_copy(
        src_ref=src, dst_ref=dst, send_sem=ssem, recv_sem=rsem, device_id=dev, device_id_type=MESH
    )
    copy.start()


def await_bytes(ref, sem):
    pltpu.make_async_copy(ref, ref, sem).wait()


def kernel(
    rows_ref, lab_ref, proj_ref, w_ref, hg_ref, out_ref,
    wf, proj, ph, ga, gb, normed, rt, rnd, logt, lg_all, r_all,
    p3, rx3, az3, af3, rz3,
    phr, pb, mgb, jb, jx, sx, sz, inv_keep,
    xch, xin, bk, bkin,
    loc_sem, w_s, w_r, l_s, l_r, r_s, r_r,
    g1s, g1r, g2s, g2r, st_s, st_r, q3s, q3r, p_s, p_r, m_s, m_r, j_s, j_r, ra_s, ra_r, x_s, x_r,
):
    s = lax.axis_index("section")
    v = lax.axis_index("vocab")
    t = lax.axis_index("tok")
    z = lax.div(v, 8)
    x = lax.rem(lax.div(v, 2), 4)
    yl = lax.rem(v, 2)
    b = s * 4 + t
    sib = {"section": 1 - s}
    t_right = lax.rem(t + 1, 4)
    t_left = lax.rem(t + 3, 4)
    t_far = lax.rem(t + 2, 4)

    def at_z(d):
        return {"vocab": lax.rem(z + d, 8) * 8 + x * 2 + yl}

    def at_x(d):
        return {"vocab": z * 8 + lax.rem(x + d, 4) * 2 + yl}

    zy = z * 2 + yl

    def vocab_of(e):
        return {"vocab": lax.div(e, 2) * 8 + x * 2 + lax.rem(e, 2)}

    def at_zy(d):
        return vocab_of(lax.rem(zy + d, 16))

    xy = x * 2 + yl

    def at_xy(d):
        return {"vocab": z * 8 + lax.rem(xy + d, 8)}

    at_y = {"vocab": z * 8 + x * 2 + (1 - yl)}

    barrier = pltpu.get_barrier_semaphore()
    for d in range(1, 16):
        pl.semaphore_signal(barrier, inc=1, device_id=at_zy(d), device_id_type=MESH)
    for d in range(1, 8):
        pl.semaphore_signal(barrier, inc=1, device_id=at_xy(d), device_id_type=MESH)
    for d in range(1, 8):
        o = lax.rem(b + d, 8)
        pl.semaphore_signal(
            barrier, inc=1, device_id={"section": lax.div(o, 4), "tok": lax.rem(o, 4)}, device_id_type=MESH
        )
    own_t = rows_ref[0].astype(F32)
    ga[z, x, yl] = jnp.concatenate([own_t, jnp.zeros((CP - C, T), F32)], axis=0).astype(BF)
    pl.semaphore_wait(barrier, 29)

    def gather_y(g, ss, rs):
        rcopy(g.at[z, x, yl], g.at[z, x, yl], ss.at[0], rs.at[0], at_y)
        await_bytes(g.at[z, x, 1 - yl], rs.at[0])

    def gather(g, ss, rs, between, direct=False):
        for d in (4, 3, 5, 2, 6, 1, 7):
            rcopy(g.at[z, x], g.at[z, x], ss.at[1], rs.at[1], at_z(d))
        between()
        await_bytes(g.at[pl.ds(0, 7), x], rs.at[1])
        if direct:
            for d in (2, 1, 3):
                rcopy(g.at[:, x], g.at[:, x], ss.at[2], rs.at[2], at_x(d))
            await_bytes(g.at[:, pl.ds(0, 3)], rs.at[2])
            return
        xl = lax.rem(x + 3, 4)
        xr = lax.rem(x + 1, 4)
        rcopy(g.at[:, x], g.at[:, x], ss.at[2], rs.at[2], at_x(1))
        rcopy(g.at[:, x], g.at[:, x], ss.at[2], rs.at[3], at_x(3))
        await_bytes(g.at[:, xl], rs.at[2])
        lo = pl.ds(0, 4)
        hi = pl.ds(4, 4)
        rcopy(g.at[lo, xl], g.at[lo, xl], ss.at[2], rs.at[4], at_x(1))
        await_bytes(g.at[:, xr], rs.at[3])
        rcopy(g.at[hi, xr], g.at[hi, xr], ss.at[2], rs.at[5], at_x(3))
        await_bytes(g.at[lo, x], rs.at[4])
        await_bytes(g.at[hi, x], rs.at[5])

    def gather_sent(g, ss):
        await_bytes(g.at[z, x, yl], ss.at[0])
        await_bytes(g.at[pl.ds(0, 7), x], ss.at[1])
        await_bytes(g.at[:, pl.ds(0, 3)], ss.at[2])

    def ring_start(own, piece, ss, rs):
        right = {"tok": t_right}
        left = {"tok": t_left}
        rcopy(own(0), piece(b, 0), ss, rs.at[0], right)
        rcopy(own(1), piece(b, 1), ss, rs.at[3], left)

    def ring_second(own, piece, ss, rs):
        right = {"tok": t_right}
        left = {"tok": t_left}
        rcopy(own(0), piece(b, 0), ss, rs.at[6], sib)
        rcopy(own(1), piece(b, 1), ss, rs.at[6], sib)
        rcopy(own(1), piece(b, 1), ss, rs.at[1], right)
        rcopy(own(0), piece(b, 0), ss, rs.at[2], left)

    def hand(piece, blk, h, ss, rs):
        rcopy(piece(blk, h), piece(blk, h), ss, rs.at[6], sib)

    def ring_mid(piece, ss, rs):
        bl = s * 4 + t_left
        br = s * 4 + t_right
        await_bytes(piece(bl, 0), rs.at[0])
        for q in range(2):
            rcopy(piece(bl, 0, q), piece(bl, 0, q), ss, rs.at[4 + 3 * q], {"tok": t_right})
        await_bytes(piece(br, 1), rs.at[3])
        for q in range(2):
            rcopy(piece(br, 1, q), piece(br, 1, q), ss, rs.at[5 + 3 * q], {"tok": t_left})
        hand(piece, bl, 0, ss, rs)
        hand(piece, br, 1, ss, rs)

    def ring_near(piece, ss, rs):
        bl = s * 4 + t_left
        br = s * 4 + t_right
        await_bytes(piece(bl, 1), rs.at[1])
        hand(piece, bl, 1, ss, rs)
        await_bytes(piece(br, 0), rs.at[2])
        hand(piece, br, 0, ss, rs)

    def ring_late(piece, ss, rs):
        bf = s * 4 + t_far
        for q in range(2):
            for h in range(2):
                await_bytes(piece(bf, h, q), rs.at[4 + h + 3 * q])
                rcopy(piece(bf, h, q), piece(bf, h, q), ss, rs.at[6], sib)

    def w_own(h):
        return w_ref.at[pl.ds(224 * h, 224), :]

    def w_piece(blk, h, q=None):
        first, count = (224 * h, 224) if q is None else (224 * h + 112 * q, 112)
        return wf.at[pl.ds(pl.multiple_of(KB * blk + first, 16), count), :]

    def l_piece(blk, h, q=None):
        first, count = (512 * h, 512) if q is None else (512 * h + 256 * q, 256)
        return lg_all.at[pl.ds(first, count), pl.ds(pl.multiple_of(blk * T, T), T)]

    def l_own(h):
        return l_piece(b, h)

    pcopy = pltpu.make_async_copy(proj_ref, proj, loc_sem.at[0])
    pcopy.start()
    gather_y(ga, g1s, g1r)
    ring_start(w_own, w_piece, w_s, w_r)

    @pl.when(s == 0)
    def _():
        ring_second(w_own, w_piece, w_s, w_r)

    wcopy = pltpu.make_async_copy(w_ref, wf.at[pl.ds(pl.multiple_of(KB * b, 64), KB), :], loc_sem.at[1])
    wcopy.start()

    def normalize(g):
        def add(i, acc):
            for j in range(8):
                blk = g[i, j // 2, j % 2][:C, :].astype(F32)
                acc = acc + (blk * blk)
            return acc

        total = lax.fori_loop(0, 8, add, jnp.zeros((C, T), F32))
        inv = lax.rsqrt(jnp.sum(total, axis=0, keepdims=True) * (1.0 / D) + EPS)

        def scale(i, carry):
            parts = [g[i, j // 2, j % 2][:C, :].astype(F32) for j in range(8)]
            block = jnp.concatenate(parts, axis=0) * inv
            r = pl.multiple_of(i * KB, KB)
            normed[pl.ds(r, KB), :] = block
            rt[pl.ds(r, KB), :] = block.astype(BF)
            return carry

        lax.fori_loop(0, 8, scale, 0)
        return inv

    def share_proj():
        pcopy.wait()

        @pl.when(s == 1)
        def _():
            odd = lax.rem(z, 2) == 1

            def turn_proj(i, carry):
                r = pl.multiple_of(i * T, T)
                block = proj[:, pl.ds(r, T)].astype(F32)
                even_place = jnp.concatenate([block, jnp.zeros((T - C, T), F32)], axis=0)
                odd_place = jnp.concatenate([jnp.zeros((CP, T), F32), block, jnp.zeros((CP - C, T), F32)], axis=0)
                ph[pl.ds(r, T), :] = jnp.where(odd, odd_place, even_place).T.astype(BF)
                return carry

            lax.fori_loop(0, D // T, turn_proj, 0)
            for d in (4, 3, 5, 2, 6, 1, 7):
                zo = lax.rem(z + d, 8)
                rcopy(ph.at[pl.ds(pl.multiple_of(zo * KB, 64), KB), :], phr.at[z], p_s, p_r, at_z(d))
            phr[z] = ph[pl.ds(pl.multiple_of(z * KB, 64), KB), :]

    gather(ga, g1s, g1r, share_proj)
    inv1 = normalize(ga)
    part = jnp.dot(proj[:, pl.ds(pl.multiple_of(s * D, D), D)], rt[...], preferred_element_type=F32)
    own_rows = pl.ds(pl.multiple_of(v * C, 8), C)

    @pl.when(s == 0)
    def _():
        xch[pl.ds(0, C), :] = part
        xch[pl.ds(C, 8), :] = jnp.broadcast_to(inv1, (8, T))
        xch[pl.ds(CP, C), :] = normed[own_rows, :]
        xch[pl.ds(CP + C, 8), :] = jnp.zeros((8, T), F32)
        rcopy(xch, xin, x_s.at[0], x_r.at[0], sib)
        inv_keep[...] = jnp.broadcast_to(inv1, (8, T))
        ring_mid(w_piece, w_s, w_r)
        ring_near(w_piece, w_s, w_r)

    @pl.when(s == 1)
    def _():
        await_bytes(xin, x_r.at[0])
        mixed = part + xin[pl.ds(0, C), :]
        gb[z, x, yl] = jnp.concatenate([mixed, jnp.zeros((CP - C, T), F32)], axis=0).astype(BF)
        rcopy(gb.at[z, x, yl], gb.at[z, x, yl], g2s.at[0], g2r.at[0], at_y)
        ring_second(w_own, w_piece, w_s, w_r)
        ring_mid(w_piece, w_s, w_r)
        await_bytes(gb.at[z, x, 1 - yl], g2r.at[0])
        gather(gb, g2s, g2r, lambda: None, direct=True)
        ring_near(w_piece, w_s, w_r)
        inv_keep[...] = jnp.broadcast_to(normalize(gb), (8, T))
        await_bytes(phr.at[pl.ds(0, 7)], p_r)
        for i in range(4):
            pb[:, pl.ds(i * T, T)] = phr[2 * i] + phr[2 * i + 1]

    ring_late(w_piece, w_s, w_r)

    def turn(i, carry):
        r = pl.multiple_of(i * T, T)
        rnd[:, pl.ds(r, T)] = normed[pl.ds(r, T), :].T.astype(BF)
        return carry

    lax.fori_loop(0, D // T, turn, 0)
    wcopy.wait()
    await_bytes(wf.at[pl.ds(0, 4 * KB), :], w_r.at[6])

    part_rows = pl.ds(pl.multiple_of(x * SHARE, 16), SHARE)
    own_tokens = pl.ds(pl.multiple_of(b * T, T), T)

    def rows_of(o):
        return pl.ds(pl.multiple_of(o * KB + x * SHARE, 16), SHARE)

    def to_owner(d, carry):
        o = lax.rem(b + d, 8)
        rcopy(
            rt.at[rows_of(o), :], r_all.at[part_rows, own_tokens],
            r_s, r_r, {"section": lax.div(o, 4), "tok": lax.rem(o, 4)},
        )
        return carry

    def share_rows():
        await_bytes(r_all.at[part_rows, pl.ds(0, 7 * T)], r_r)
        for d in (2, 1, 3):
            rcopy(r_all.at[part_rows, :], r_all.at[part_rows, :], ra_s, ra_r, at_x(d))

    def logits_tile(i, carry):
        r = pl.multiple_of(i * 256, 256)
        tile = jnp.dot(rnd[...], wf[:, pl.ds(r, 256)], preferred_element_type=F32)
        logt[pl.ds(r, 256), :] = tile.T
        return carry

    lax.fori_loop(0, 4, logits_tile, 0)
    r_all[part_rows, own_tokens] = rt[rows_of(b), :]

    label = lab_ref[...] - v * VS
    place = lax.broadcasted_iota(jnp.int32, (VS, T), 0)
    hit = place == label
    values = logt[...]
    top = jnp.max(values, axis=0, keepdims=True)
    expo = jnp.exp(values - top)
    den = jnp.sum(expo, axis=0, keepdims=True)
    sel = jnp.sum(expo * values, axis=0, keepdims=True)
    lab = jnp.sum(jnp.where(hit, values, 0.0), axis=0, keepdims=True)

    def combine(slots):
        m = slots[0][0:1]
        for q in slots[1:]:
            m = jnp.maximum(m, q[0:1])
        d_ = jnp.zeros((1, T), F32)
        e_ = jnp.zeros((1, T), F32)
        l_ = jnp.zeros((1, T), F32)
        for q in slots:
            f = jnp.exp(q[0:1] - m)
            d_ = d_ + q[1:2] * f
            e_ = e_ + q[2:3] * f
            l_ = l_ + q[3:4]
        return jnp.concatenate([m, d_, e_, l_, jnp.zeros((4, T), F32)], axis=0)

    sx[xy] = jnp.concatenate([top, den, sel, lab, jnp.zeros((4, T), F32)], axis=0)
    for d in (4, 5, 3, 1, 7, 2, 6):
        rcopy(sx.at[xy], sx.at[xy], st_s.at[0], st_r.at[0], at_xy(d))
    lax.fori_loop(1, 8, to_owner, 0)
    await_bytes(sx.at[pl.ds(0, 7)], st_r.at[0])
    sz[z] = combine([sx[i] for i in range(8)])
    for d in (4, 3, 5, 2, 6, 1, 7):
        rcopy(sz.at[z], sz.at[z], st_s.at[1], st_r.at[1], at_z(d))
    await_bytes(sz.at[pl.ds(0, 7)], st_r.at[1])
    stats = combine([sz[i] for i in range(8)])
    weighting = jnp.where(s == 1, MTP_WEIGHT, 1.0).astype(F32)
    inv_den = 1.0 / stats[1:2]
    mean_dot = weighting * (stats[2:3] * inv_den - stats[3:4]) * (1.0 / D)
    prob = jnp.exp(logt[...] - stats[0:1]) * inv_den
    lgt = (weighting * (prob - hit.astype(F32))).astype(BF)
    lg_all[:, pl.ds(pl.multiple_of(b * T, T), T)] = lgt

    ring_start(l_own, l_piece, l_s, l_r)

    @pl.when(s == 0)
    def _():
        ring_second(l_own, l_piece, l_s, l_r)

    pad = jnp.zeros((CP - C, T), F32)

    def spread(block, p, i):
        for j in range(8):
            p[i, j // 2, j % 2] = jnp.concatenate([block[C * j:C * (j + 1), :], pad], axis=0).astype(BF)

    def group(d):
        return lax.rem(lax.div(z, GROUP) + d, GROUPS)

    def blocks(d):
        return pl.ds(pl.multiple_of(group(d) * GROUP, GROUP), GROUP)

    def scatter_x(make, p, rx, ss, rs):
        for n in range(GROUPS):
            d = GROUPS - 1 - n
            for k in range(GROUP):
                make(group(d) * GROUP + k)
            for dx in (2, 1, 3):
                xo = lax.rem(x + dx, 4)
                rcopy(p.at[blocks(d), xo], rx.at[x, blocks(d)], ss, rs.at[d], at_x(dx))

    def scatter_zy(p, rx, az, af, rz, ss, rs, ss2, rs2):
        for n in range(GROUPS):
            d = GROUPS - 1 - n
            await_bytes(rx.at[pl.ds(0, 3), blocks(d)], rs.at[d])
            for k in range(GROUP):
                i = group(d) * GROUP + k
                for j in range(2):
                    a = p[i, x, j].astype(F32)
                    for dx in range(1, 4):
                        a = a + rx[lax.rem(x + dx, 4), i, j].astype(F32)
                    e = i * 2 + j
                    af[e] = a
                    az[e] = a.astype(BF)

                    @pl.when(e != zy)
                    def _():
                        rcopy(az.at[e], rz.at[zy], ss2, rs2, vocab_of(e))
        @pl.when(s == 1)
        def _():
            ring_second(l_own, l_piece, l_s, l_r)

        ring_mid(l_piece, l_s, l_r)
        share_rows()
        await_bytes(rz.at[pl.ds(0, 15)], rs2)
        a = af[zy]
        for d in range(1, 16):
            a = a + rz[lax.rem(zy + d, 16)].astype(F32)
        return a[:C, :]

    def scatter_sent(rx, rz, ss, ss2):
        await_bytes(rx.at[pl.ds(0, 3)], ss)
        await_bytes(rz.at[pl.ds(0, 15)], ss2)

    def feature(i):
        block = jnp.dot(wf[pl.ds(pl.multiple_of(i * KB, KB), KB), :], lgt, preferred_element_type=F32)
        spread(block, p3, i)

    scatter_x(feature, p3, rx3, q3s.at[0], q3r)
    fgrad = scatter_zy(p3, rx3, az3, af3, rz3, q3s.at[0], q3r, q3s.at[1], q3r.at[8])
    back = (fgrad - normed[own_rows, :] * mean_dot) * inv_keep[0:1]

    def head_grad():
        await_bytes(r_all.at[pl.ds(0, 3 * SHARE), :], ra_r)
        ring_near(l_piece, l_s, l_r)
        ring_late(l_piece, l_s, l_r)
        await_bytes(lg_all.at[:, pl.ds(0, 4 * T)], l_r.at[6])

        def tile(i, carry):
            r = pl.multiple_of(i * 256, 256)
            g = lax.dot_general(
                r_all[...], lg_all[pl.ds(r, 256), :], (((1,), (1,)), ((), ())), preferred_element_type=F32
            )
            hg_ref[:, pl.ds(r, 256)] = g.astype(BF)
            return carry

        lax.fori_loop(0, 4, tile, 0)

    @pl.when(s == 0)
    def _():
        bk[...] = back
        rcopy(bk, bkin, x_s.at[1], x_r.at[1], sib)
        head_grad()
        await_bytes(bkin, x_r.at[1])
        out_ref[...] = back + bkin[...]
        await_bytes(xch, x_s.at[0])

    @pl.when(s == 1)
    def _():
        mg = back.astype(BF)
        hdot = jnp.sum(mg.astype(F32) * xin[pl.ds(0, C), :], axis=0, keepdims=True)
        high = hdot.astype(BF).astype(F32)
        middle = (hdot - high).astype(BF).astype(F32)
        low = hdot - high - middle
        mgb[z] = jnp.concatenate(
            [mg.astype(F32), high, middle, low, jnp.zeros((5, T), F32)], axis=0
        ).astype(BF)
        for d in (4, 3, 5, 2, 6, 1, 7):
            rcopy(mgb.at[z], mgb.at[z], m_s, m_r, at_z(d))
        await_bytes(mgb.at[pl.ds(0, 7)], m_r)
        hsum = jnp.zeros((8, T), F32)
        for i in range(8):
            hsum = hsum + mgb[i, pl.ds(C - 8, 16), :].astype(F32)[8:16]
        hrow = hsum[0:1] + hsum[1:2] + hsum[2:3]
        joint = jnp.dot(pb[...], mgb[...].reshape(8 * CP, T), preferred_element_type=F32)
        for j in range(8):
            jb[j] = jnp.concatenate([joint[C * j:C * (j + 1), :], jnp.broadcast_to(hrow, (8, T))], axis=0)
        for d in (4, 5, 3, 1, 7, 2, 6):
            rcopy(jb.at[lax.rem(xy + d, 8)], jx.at[xy], j_s, j_r, at_xy(d))
        await_bytes(jx.at[pl.ds(0, 7)], j_r)
        tot = jb[xy]
        for d in range(1, 8):
            tot = tot + jx[lax.rem(xy + d, 8)]
        jgrad = tot[:C, :]
        hmean = tot[C:C + 1] * (1.0 / D)
        depth = (jgrad - xin[pl.ds(CP, C), :] * hmean) * xin[pl.ds(C, 1), :]
        bk[...] = depth
        rcopy(bk, bkin, x_s.at[1], x_r.at[1], sib)
        await_bytes(bkin, x_r.at[1])
        out_ref[...] = bkin[...] + depth
        head_grad()
        gather_sent(gb, g2s)
        await_bytes(mgb.at[pl.ds(0, 7)], m_s)
        await_bytes(jx.at[pl.ds(0, 7)], j_s)
        await_bytes(phr.at[pl.ds(0, 7)], p_s)

    await_bytes(bk, x_s.at[1])
    gather_sent(ga, g1s)
    scatter_sent(rx3, rz3, q3s.at[0], q3s.at[1])
    await_bytes(sx.at[pl.ds(0, 7)], st_s.at[0])
    await_bytes(sz.at[pl.ds(0, 7)], st_s.at[1])
    await_bytes(r_all.at[part_rows, pl.ds(0, 7 * T)], r_s)
    await_bytes(r_all.at[pl.ds(0, 3 * SHARE), :], ra_s)
    await_bytes(wf.at[pl.ds(0, 7 * KB), :], w_s)
    await_bytes(lg_all.at[:, pl.ds(0, 7 * T)], l_s)


def local(rows, targets, proj_weight, head_weight):
    vm = pl.BlockSpec(memory_space=pltpu.VMEM)
    anyspace = pl.BlockSpec(memory_space=pl.ANY)
    dma = pltpu.SemaphoreType.DMA

    def rs_bufs():
        return [
            pltpu.VMEM((8, 4, 2, CP, T), BF),
            pltpu.VMEM((4, 8, 2, CP, T), BF),
            pltpu.VMEM((16, CP, T), BF),
            pltpu.VMEM((16, CP, T), F32),
            pltpu.VMEM((16, CP, T), BF),
        ]

    head_grad, grad_t = pl.pallas_call(
        kernel,
        out_shape=(
            jax.ShapeDtypeStruct((KB, VS), BF),
            jax.ShapeDtypeStruct((C, T), F32),
        ),
        in_specs=[vm, vm, anyspace, anyspace],
        out_specs=(vm, vm),
        scratch_shapes=[
            pltpu.VMEM((D, VS), BF),
            pltpu.VMEM((C, 2 * D), BF),
            pltpu.VMEM((D, T), BF),
            pltpu.VMEM((8, 4, 2, CP, T), BF),
            pltpu.VMEM((8, 4, 2, CP, T), BF),
            pltpu.VMEM((D, T), F32),
            pltpu.VMEM((D, T), BF),
            pltpu.VMEM((T, D), BF),
            pltpu.VMEM((VS, T), F32),
            pltpu.VMEM((VS, 8 * T), BF),
            pltpu.VMEM((KB, 8 * T), BF),
            *rs_bufs(),
            pltpu.VMEM((8, KB, T), BF),
            pltpu.VMEM((KB, 8 * CP), BF),
            pltpu.VMEM((8, CP, T), BF),
            pltpu.VMEM((8, CP, T), F32),
            pltpu.VMEM((8, CP, T), F32),
            pltpu.VMEM((8, 8, T), F32),
            pltpu.VMEM((8, 8, T), F32),
            pltpu.VMEM((8, T), F32),
            pltpu.VMEM((2 * CP, T), F32),
            pltpu.VMEM((2 * CP, T), F32),
            pltpu.VMEM((C, T), F32),
            pltpu.VMEM((C, T), F32),
            dma((2,)), dma, dma((9,)), dma, dma((9,)), dma, dma,
            dma((3,)), dma((6,)), dma((3,)), dma((6,)),
            dma((2,)), dma((2,)), dma((2,)), dma((9,)),
            dma, dma, dma, dma, dma, dma, dma, dma,
            dma((2,)), dma((2,)),
        ],
        compiler_params=pltpu.CompilerParams(
            collective_id=0, has_side_effects=True, vmem_limit_bytes=56 * 1024 * 1024
        ),
        cost_estimate=pl.CostEstimate(flops=3 * 10**9, bytes_accessed=2 * 10**7, transcendentals=3 * 10**5),
        name="head",
    )(jnp.swapaxes(rows, 1, 2), targets, proj_weight.T, head_weight)
    return head_grad, grad_t.T


def solution(mesh):
    placed = (
        P("section", "tok", "vocab"),
        P("section", "tok"),
        P(None, "vocab"),
        P(("section", "tok"), "vocab"),
    )
    return jax.shard_map(
        local,
        mesh=mesh,
        in_specs=placed,
        out_specs=(P(("section", "tok"), "vocab"), P("tok", "vocab")),
        check_vma=False,
    )
```
